512 devices in a mesh: ctx: 64 (over z, x_hi, core), head: 8 (over y, x_lo).
Axes of the slice: x: 4 (x_hi: 2, x_lo: 2; x = x_hi * 2 + x_lo), y: 4, z: 16, core: 2. Of those that a mesh axis runs over, the one named last changes fastest.
Arguments:
- queries: bfloat16 [8192, 8192], P('ctx', 'head'), may hold values from -6 to 6
- q_gain: float32 [128], replicated, may hold values from 0.5 to 2.5
- k_gain: float32 [128], replicated, may hold values from 0.5 to 2.5
- attn_gate: float32 [1], replicated, may hold values from 0.3 to 1.5
- vision: bfloat16 [8192, 8192], P('ctx', 'head'), may hold values from -6 to 6
- key_projection_matrix: bfloat16 [8192, 1024], P('ctx', 'head'), may hold values from -0.0625 to 0.0625
- value_projection_matrix: bfloat16 [8192, 1024], P('ctx', 'head'), may hold values from -0.0625 to 0.0625
- image_start: int32 [24], replicated, may hold values from 1 to 8191, as said below
- slot_image: int32 [128], replicated, may hold values from 0 to 24, as said below
Outputs:
- attended: bfloat16 [8192, 8192], P('ctx', 'head')
The draws below stay inside these ranges and needn't reach their ends.
Inputs may be any that keep to these rules, and one draw needn't show every extreme that they name: `image_start`: strictly increasing; the first image stands at position 1 and the last at 8191. `slot_image`: value 24 marks an empty slot. Each image has 3 to 4 tiles and some image exactly 4. Used slots are each device's lowest slots, and the numbers of used slots of two devices differ by at most one.
All inputs are finite; a program needn't handle non-finite values.
Results may differ from the reference program's by a relative error of at most 0.011.
Values may be sent and summed in bfloat16 or wider, within the bound.
No kernel may reach another device: no remote copies, remote signals or barrier semaphores. Data moves between devices by JAX's collectives and lax.ppermute only.
A program may use at most 64 MiB of HBM per device.

```python
import math
import jax
import jax.numpy as jnp
from jax import lax

MODEL_WIDTH = 8192
QUERY_HEADS = 64
KEY_VALUE_HEADS = 8
HEAD_SIZE = 128
SLOTS_DEV = 2
TILE_TOK = 64
TOKENS = 8192
SLOTS = 128
IMAGES = 24


def draw_image_start(key, part):
    key = jax.random.fold_in(key, 11)
    inner = jax.random.permutation(key, TOKENS - 3)[:IMAGES - 2].astype(jnp.int32) + 2
    starts = jnp.concatenate([jnp.array([1], jnp.int32), inner, jnp.array([TOKENS - 1], jnp.int32)])
    return jnp.sort(starts).astype(jnp.int32)


def draw_slot_image(key, part):
    key = jax.random.fold_in(key, 23)
    key_counts, key_full, key_order = jax.random.split(key, 3)
    counts = jax.random.randint(key_counts, (IMAGES,), 3, 5).astype(jnp.int32)
    full_one = jax.random.randint(key_full, (), 0, IMAGES)
    counts = jnp.where(jnp.arange(IMAGES, dtype=jnp.int32) == full_one, 4, counts).astype(jnp.int32)
    ends = jnp.cumsum(counts).astype(jnp.int32)
    total = ends[-1]
    index = jnp.arange(SLOTS, dtype=jnp.int32)
    tile_image = jnp.sum((ends[None, :] <= index[:, None]).astype(jnp.int32), axis=1).astype(jnp.int32)
    ranks = jax.random.permutation(key_order, SLOTS).astype(jnp.int32) + jnp.where(index >= total, SLOTS, 0).astype(jnp.int32)
    order = jnp.argsort(ranks)
    shuffled = tile_image[order]
    ctx_count = SLOTS // SLOTS_DEV
    target = index % ctx_count * SLOTS_DEV + index // ctx_count
    return jnp.zeros((SLOTS,), jnp.int32).at[target].set(shuffled)


def block_levels(own_key, shape, shards, least, high):
    def one(axis_at, blocks):
        steps = jax.random.uniform(jax.random.fold_in(jax.random.fold_in(own_key, 6), axis_at), (blocks,), jnp.float32, least / len(shards), high / len(shards))
        return jnp.repeat(jnp.exp(steps), shape[axis_at] // blocks).reshape((-1,) + (1,) * (len(shape) - axis_at - 1))

    level = one(*shards[0])
    for cut in shards[1:]:
        level = level * one(*cut)
    return level


def bell_draw(own_key, extent, width, most, cuts=(), kind=jnp.bfloat16):
    values = width * jax.random.normal(own_key, extent, jnp.float32)
    if cuts:
        values = values * block_levels(own_key, extent, cuts, -0.22, 0.18)
    return jnp.clip(values, -most, most).astype(kind)


def setup_inputs(seed: int = 0) -> dict:
    streams_of = jax.random.split(jax.random.key(seed), 10)
    queries = bell_draw(streams_of[0], (TOKENS, QUERY_HEADS * HEAD_SIZE), 1.0, 6.0, ((0, 64), (1, 8)))
    q_gain = jnp.clip(jax.random.uniform(streams_of[1], (HEAD_SIZE,), jnp.float32, 0.5, 2.5), 0.5, 2.5)
    k_gain = jnp.clip(jax.random.uniform(streams_of[2], (HEAD_SIZE,), jnp.float32, 0.5, 2.5), 0.5, 2.5)
    attn_gate = jnp.clip(jax.random.uniform(streams_of[3], (1,), jnp.float32, 0.3, 1.5), 0.3, 1.5)
    vision = bell_draw(streams_of[4], (SLOTS * TILE_TOK, MODEL_WIDTH), 1.0, 6.0, ((0, 64), (1, 8)))
    key_projection_matrix = bell_draw(streams_of[5], (MODEL_WIDTH, KEY_VALUE_HEADS * HEAD_SIZE), MODEL_WIDTH ** -0.5, 0.0625, ((0, 64), (1, 8)))
    value_projection_matrix = bell_draw(streams_of[6], (MODEL_WIDTH, KEY_VALUE_HEADS * HEAD_SIZE), MODEL_WIDTH ** -0.5, 0.0625, ((0, 64), (1, 8)))
    image_start = draw_image_start(jax.random.fold_in(streams_of[9], 71), 0)
    slot_image = draw_slot_image(jax.random.fold_in(streams_of[9], 71), 0)
    return {"queries": queries, "q_gain": q_gain, "k_gain": k_gain, "attn_gate": attn_gate, "vision": vision, "key_projection_matrix": key_projection_matrix, "value_projection_matrix": value_projection_matrix, "image_start": image_start, "slot_image": slot_image}


EPS = 1e-05

def rms_scale(raw, gain):
    return raw * lax.rsqrt(lax.optimization_barrier(jnp.mean(raw * raw, axis=-1, keepdims=True)) + EPS) * gain

def reference(queries, q_gain, k_gain, attn_gate, vision, key_projection_matrix, value_projection_matrix, image_start, slot_image):
    vision_rows = SLOTS * TILE_TOK
    head_group = QUERY_HEADS // KEY_VALUE_HEADS
    unnormed_keys = jnp.dot(vision, key_projection_matrix, preferred_element_type=jnp.float32).reshape(vision_rows, KEY_VALUE_HEADS, HEAD_SIZE)
    keys = rms_scale(unnormed_keys, k_gain).astype(jnp.bfloat16)
    value_vectors = jnp.dot(vision, value_projection_matrix, preferred_element_type=jnp.float32).astype(jnp.bfloat16).reshape(vision_rows, KEY_VALUE_HEADS, HEAD_SIZE)
    normalized_input = rms_scale(queries.astype(jnp.float32).reshape(TOKENS, QUERY_HEADS, HEAD_SIZE), q_gain).astype(jnp.bfloat16)
    match = slot_image[:, None] == jnp.arange(IMAGES, dtype=jnp.int32)[None, :]
    slot_start = lax.optimization_barrier(jnp.sum(jnp.where(match, image_start[None, :], 0), axis=1)) + jnp.where(slot_image >= IMAGES, TOKENS, 0)
    row_begin = jnp.repeat(slot_start.astype(jnp.int32), TILE_TOK)
    rows_per_block = math.gcd(TOKENS, 256)
    block_list = TOKENS // rows_per_block
    grouped_heads = normalized_input.reshape(block_list, rows_per_block, KEY_VALUE_HEADS, head_group, HEAD_SIZE).transpose(2, 0, 1, 3, 4)
    positions = jnp.arange(TOKENS, dtype=jnp.int32).reshape(block_list, rows_per_block)
    scale = HEAD_SIZE ** (-0.5)
    factor = jnp.tanh(attn_gate[0])

    def one_head(head_args):
        query_head, key_head, value_head = head_args
        key_float = key_head.astype(jnp.float32)
        value_float = value_head.astype(jnp.float32)

        def one_block(block_args):
            query_block, position = block_args
            scores = jnp.einsum('qgd,vd->qgv', query_block.astype(jnp.float32), key_float) * scale
            visible = (row_begin[None, :] <= position[:, None])[:, None, :]
            weights = jnp.where(visible, jnp.exp(scores), 0.0)
            denom = lax.optimization_barrier(jnp.sum(weights, axis=-1))
            rounded = lax.optimization_barrier(weights.astype(jnp.bfloat16))
            numer = jnp.einsum('qgv,vd->qgd', rounded.astype(jnp.float32), value_float)
            seen_row = position >= image_start[0]
            safe = jnp.where(seen_row[:, None], denom, 1.0)[:, :, None]
            return jnp.where(seen_row[:, None, None], factor * numer / safe, 0.0).astype(jnp.bfloat16)
        return lax.map(one_block, (query_head, positions))
    result = lax.map(one_head, (grouped_heads, keys.transpose(1, 0, 2), value_vectors.transpose(1, 0, 2)))
    return result.transpose(1, 2, 0, 3, 4).reshape(TOKENS, QUERY_HEADS * HEAD_SIZE)
```

```python
import functools
import math

import jax
import jax.numpy as jnp
from jax import lax
from jax.experimental import pallas as pl
from jax.experimental.pallas import tpu as pltpu
from jax.sharding import PartitionSpec as P

EPS = 1e-05
PLANE = 4
VMEM_LIMIT = 48 * 1024 * 1024


def params(**more):
    return pltpu.CompilerParams(vmem_limit_bytes=VMEM_LIMIT, **more)


def vmem():
    return pl.BlockSpec(memory_space=pltpu.VMEM)


def smem():
    return pl.BlockSpec(memory_space=pltpu.SMEM)


def project_kernel(x_ref, w_ref, out_ref):
    members, pieces, rows, depth = x_ref.shape
    total = None
    for piece in range(pieces):
        part = jnp.dot(
            x_ref[:, piece].reshape(members * rows, depth),
            w_ref[piece],
            preferred_element_type=jnp.float32,
        )
        total = part if total is None else total + part
    out_ref[...] = total.reshape(out_ref.shape).astype(out_ref.dtype)


def finish_kernel(parts_ref, gain_ref, out_ref):
    raw = jnp.sum(parts_ref[...].astype(jnp.float32), axis=0)
    head_dim = gain_ref.shape[1]
    keys = raw[:, :head_dim]
    mean = jnp.mean(keys * keys, axis=-1, keepdims=True)
    keys = keys * lax.rsqrt(mean + EPS) * gain_ref[...]
    both = jnp.concatenate([keys, raw[:, head_dim:]], axis=1).astype(out_ref.dtype)
    for copy in range(out_ref.shape[0]):
        out_ref[copy] = both


def query_kernel(q_ref, gain_ref, out_ref):
    heads, _, head_dim = out_ref.shape
    for head in range(heads):
        raw = q_ref[:, head * head_dim : (head + 1) * head_dim].astype(jnp.float32)
        mean = jnp.mean(raw * raw, axis=-1, keepdims=True)
        out_ref[head] = (raw * lax.rsqrt(mean + EPS) * gain_ref[...]).astype(out_ref.dtype)


def attend_kernel(
    image_start_ref,
    slot_image_ref,
    place_ref,
    q_ref,
    kv_ref,
    out_ref,
    keys_ref,
    values_ref,
    begin_ref,
    total_ref,
    *,
    scale,
    group,
    slots_here,
):
    slots, tile_rows, width = kv_ref.shape
    heads, tokens, head_dim = q_ref.shape
    members, own, _ = out_ref.shape
    n_images = image_start_ref.shape[0]
    plane_rank = place_ref[0]
    member = place_ref[1]
    first_token = plane_rank * tokens
    total_tokens = (slots // slots_here) * tokens
    limit = first_token + tokens
    ones = jnp.ones((tile_rows, head_dim), jnp.bfloat16)

    def take(place, kept):
        rank = place // slots_here
        slot = (rank * PLANE + member) * slots_here + place % slots_here
        image = slot_image_ref[slot]
        start = image_start_ref[jnp.minimum(image, n_images - 1)]
        begin = jnp.where(image < n_images, start, total_tokens)

        @pl.when(begin < limit)
        def _():
            keys_ref[kept] = kv_ref[place, :, :head_dim]
            values_ref[kept] = jnp.concatenate([kv_ref[place, :, head_dim:], ones], axis=1)
            begin_ref[kept] = begin

        return kept + (begin < limit).astype(jnp.int32)

    kept = lax.fori_loop(0, slots, take, jnp.int32(0))
    turns = (kept + group - 1) // group

    def fill(place, _):
        keys_ref[place] = kv_ref[0, :, :head_dim]
        values_ref[place] = jnp.concatenate([kv_ref[0, :, head_dim:], ones], axis=1)
        begin_ref[place] = total_tokens
        return 0

    lax.fori_loop(kept, turns * group, fill, 0)
    total_ref[...] = jnp.zeros_like(total_ref)

    count = group * tile_rows
    lane = lax.broadcasted_iota(jnp.int32, (1, count), 1)
    position = first_token + lax.broadcasted_iota(jnp.int32, (tokens, 1), 0)

    def turn(number, _):
        base = number * group
        row_begin = jnp.zeros((1, count), jnp.int32)
        for place in range(group):
            row_begin = jnp.where(lane >= place * tile_rows, begin_ref[base + place], row_begin)
        keys = keys_ref[pl.ds(base, group)].reshape(count, head_dim)
        values = values_ref[pl.ds(base, group)].reshape(count, 2 * head_dim)
        visible = row_begin <= position

        def one_head(head, _):
            scores = lax.dot_general(
                q_ref[head],
                keys,
                (((1,), (1,)), ((), ())),
                preferred_element_type=jnp.float32,
            )
            weights = jnp.where(visible, jnp.exp2(scores * scale), 0.0)
            total_ref[head] += jnp.dot(
                weights.astype(jnp.bfloat16), values, preferred_element_type=jnp.float32
            )
            return 0

        lax.fori_loop(0, heads, one_head, 0)
        return 0

    lax.fori_loop(0, turns, turn, 0)

    column = lax.broadcasted_iota(jnp.int32, (own, head_dim), 1)
    for to in range(members):
        rows = slice(to * own, (to + 1) * own)
        sums = jnp.zeros((own, head_dim), jnp.float32)
        for head in range(heads):
            columns = slice(head * head_dim, (head + 1) * head_dim)
            out_ref[to, :, columns] = total_ref[head, rows, :head_dim].astype(out_ref.dtype)
            denom = total_ref[head, rows, head_dim:]
            high = denom.astype(jnp.bfloat16).astype(jnp.float32)
            sums = jnp.where(column == head, high, sums)
            sums = jnp.where(column == heads + head, denom - high, sums)
        out_ref[to, :, heads * head_dim :] = sums.astype(out_ref.dtype)


def combine_kernel(image_start_ref, place_ref, gate_ref, parts_ref, out_ref):
    members, own, width = parts_ref.shape
    plane_rank = place_ref[0]
    member = place_ref[1]
    out_width = out_ref.shape[1]
    head_dim = width - out_width
    heads = out_width // head_dim
    first = (plane_rank * members + member) * own
    position = first + lax.broadcasted_iota(jnp.int32, (own, 1), 0)
    seen = position >= image_start_ref[0]
    factor = jnp.tanh(gate_ref[...])
    sums = jnp.sum(parts_ref[:, :, out_width:].astype(jnp.float32), axis=0)
    for head in range(heads):
        columns = slice(head * head_dim, (head + 1) * head_dim)
        denom = sums[:, head : head + 1] + sums[:, heads + head : heads + head + 1]
        safe = jnp.where(seen, denom, 1.0)
        numer = jnp.sum(parts_ref[:, :, columns].astype(jnp.float32), axis=0)
        out_ref[:, columns] = jnp.where(seen, factor * numer / safe, 0.0).astype(out_ref.dtype)


def local(
    queries,
    q_gain,
    k_gain,
    attn_gate,
    vision,
    key_projection_matrix,
    value_projection_matrix,
    image_start,
    slot_image,
):
    ctx_size = lax.axis_size("ctx")
    head_size = lax.axis_size("head")
    ranks = ctx_size // PLANE
    own_index = lax.axis_index("ctx")
    plane_rank = own_index // PLANE
    member = own_index % PLANE
    place = jnp.stack([plane_rank, member]).astype(jnp.int32)
    head_dim = q_gain.shape[0]
    tokens, q_cols = queries.shape
    heads = q_cols // head_dim
    rows, features = vision.shape
    piece_rows, kv_cols = key_projection_matrix.shape
    along_z = [[rank * PLANE + m for rank in range(ranks)] for m in range(PLANE)]
    in_plane = [[rank * PLANE + m for m in range(PLANE)] for rank in range(ranks)]
    whole_plane = [
        [rank * PLANE * head_size + i for i in range(PLANE * head_size)] for rank in range(ranks)
    ]

    with jax.named_scope("gather_queries"):
        all_queries = lax.all_gather(
            queries, "ctx", axis_index_groups=in_plane, axis=0, tiled=True
        )

    with jax.named_scope("gather_projections"):
        weights = jnp.concatenate([key_projection_matrix, value_projection_matrix], axis=1)
        weights = jnp.broadcast_to(weights[None], (ranks,) + weights.shape)
        weights = lax.all_to_all(weights, "ctx", 0, 0, axis_index_groups=along_z)

    with jax.named_scope("spread_vision"):
        blocks = features // (piece_rows * PLANE)
        mine = vision.reshape(rows, blocks, PLANE, piece_rows).transpose(2, 0, 1, 3)
        mine = mine.reshape(PLANE, 1, rows, blocks * piece_rows)
        mine = jnp.broadcast_to(mine, (PLANE, head_size, rows, blocks * piece_rows))
        mine = mine.reshape(PLANE * head_size, rows, blocks * piece_rows)
        spread = lax.all_to_all(mine, ("ctx", "head"), 0, 0, axis_index_groups=whole_plane)

    with jax.named_scope("project"):
        partial = pl.pallas_call(
            project_kernel,
            out_shape=jax.ShapeDtypeStruct((PLANE, rows, 2 * kv_cols), jnp.bfloat16),
            in_specs=[vmem(), vmem()],
            out_specs=vmem(),
            compiler_params=params(),
        )(
            spread.reshape(PLANE, head_size, rows, blocks * piece_rows),
            weights.reshape(head_size, blocks * piece_rows, 2 * kv_cols),
        )

    with jax.named_scope("sum_projections"):
        partial = lax.all_to_all(partial, "ctx", 0, 0, axis_index_groups=in_plane)
        own_kv = pl.pallas_call(
            finish_kernel,
            out_shape=jax.ShapeDtypeStruct((ranks, rows, 2 * kv_cols), jnp.bfloat16),
            in_specs=[vmem(), vmem()],
            out_specs=vmem(),
            compiler_params=params(),
        )(partial, k_gain.reshape(1, head_dim))

    with jax.named_scope("gather_keys_values"):
        all_kv = lax.all_to_all(own_kv, "ctx", 0, 0, axis_index_groups=along_z)

    with jax.named_scope("norm_queries"):
        normed = pl.pallas_call(
            query_kernel,
            out_shape=jax.ShapeDtypeStruct((heads, PLANE * tokens, head_dim), jnp.bfloat16),
            in_specs=[vmem(), vmem()],
            out_specs=vmem(),
            compiler_params=params(),
        )(all_queries, q_gain.reshape(1, head_dim))

    with jax.named_scope("attend"):
        slots_here = slot_image.shape[0] // ctx_size
        tile_rows = rows // slots_here
        slots = ranks * slots_here
        group = math.gcd(slots, 8)
        packed = pl.pallas_call(
            functools.partial(
                attend_kernel,
                scale=head_dim ** (-0.5) * math.log2(math.e),
                group=group,
                slots_here=slots_here,
            ),
            out_shape=jax.ShapeDtypeStruct((PLANE, tokens, q_cols + head_dim), jnp.bfloat16),
            in_specs=[smem(), smem(), smem(), vmem(), vmem()],
            out_specs=vmem(),
            scratch_shapes=[
                pltpu.VMEM((slots, tile_rows, head_dim), jnp.bfloat16),
                pltpu.VMEM((slots, tile_rows, 2 * head_dim), jnp.bfloat16),
                pltpu.SMEM((slots,), jnp.int32),
                pltpu.VMEM((heads, PLANE * tokens, 2 * head_dim), jnp.float32),
            ],
            compiler_params=params(),
        )(
            image_start,
            slot_image,
            place,
            normed,
            all_kv.reshape(slots, tile_rows, 2 * kv_cols),
        )

    with jax.named_scope("sum_attention"):
        packed = lax.all_to_all(packed, "ctx", 0, 0, axis_index_groups=in_plane)
        return pl.pallas_call(
            combine_kernel,
            out_shape=jax.ShapeDtypeStruct((tokens, q_cols), jnp.bfloat16),
            in_specs=[smem(), smem(), vmem(), vmem()],
            out_specs=vmem(),
            compiler_params=params(),
        )(image_start, place, attn_gate.reshape(1, 1), packed)


def solution(mesh):
    in_specs = (
        P("ctx", "head"),
        P(),
        P(),
        P(),
        P("ctx", "head"),
        P("ctx", "head"),
        P("ctx", "head"),
        P(),
        P(),
    )
    out_specs = P("ctx", "head")
    return jax.shard_map(local, mesh=mesh, in_specs=in_specs, out_specs=out_specs, check_vma=False)
```

```python
import functools
import math

import jax
import jax.numpy as jnp
from jax import lax
from jax.experimental import pallas as pl
from jax.experimental.pallas import tpu as pltpu
from jax.sharding import PartitionSpec as P

EPS = 1e-05
PLANE = 4
VMEM_LIMIT = 48 * 1024 * 1024
OFFSETS = ((-4, 0, 4, 8), (-5, -1, 3, 7), (-3, 1, 5, 9), (-6, -2), (2, 6))


def params(**more):
    return pltpu.CompilerParams(vmem_limit_bytes=VMEM_LIMIT, **more)


def vmem():
    return pl.BlockSpec(memory_space=pltpu.VMEM)


def smem():
    return pl.BlockSpec(memory_space=pltpu.SMEM)


def spread_kernel(x_ref, out_ref):
    members, peers, blocks, _, width = out_ref.shape
    for member in range(members):
        for block in range(blocks):
            first = (block * members + member) * width
            piece = x_ref[:, first : first + width]
            for peer in range(peers):
                out_ref[member, peer, block] = piece


def project_kernel(place_ref, x_ref, *refs):
    weight_refs, out_ref, all_ref = refs[:-2], refs[-2], refs[-1]
    ranks, depth, width = all_ref.shape
    members, peers, blocks, rows, _ = x_ref.shape
    head_dim = width // 2
    for ref, offsets in zip(weight_refs, OFFSETS):
        for at, offset in enumerate(offsets):
            all_ref[lax.rem(place_ref[0] + offset + ranks, ranks)] = ref[at]
    total = None
    for peer in range(peers):
        for block in range(blocks):
            part = jnp.dot(
                x_ref[:, peer, block].reshape(members * rows, depth),
                all_ref[peer * blocks + block],
                preferred_element_type=jnp.float32,
            )
            total = part if total is None else total + part
    keys = total[:, :head_dim]
    high = keys.astype(jnp.bfloat16)
    low = (keys - high.astype(jnp.float32)).astype(jnp.bfloat16)
    values = total[:, head_dim:].astype(jnp.bfloat16)
    out_ref[...] = jnp.concatenate([high, low, values], axis=1).reshape(out_ref.shape)


def finish_kernel(parts_ref, gain_ref, out_ref):
    raw = jnp.sum(parts_ref[...].astype(jnp.float32), axis=0)
    head_dim = gain_ref.shape[1]
    keys = raw[:, :head_dim] + raw[:, head_dim : 2 * head_dim]
    mean = jnp.mean(keys * keys, axis=-1, keepdims=True)
    keys = keys * lax.rsqrt(mean + EPS) * gain_ref[...]
    out_ref[...] = jnp.concatenate([keys, raw[:, 2 * head_dim :]], axis=1).astype(out_ref.dtype)


def query_kernel(q_ref, gain_ref, out_ref):
    heads, _, head_dim = out_ref.shape
    for head in range(heads):
        raw = q_ref[:, head * head_dim : (head + 1) * head_dim].astype(jnp.float32)
        mean = jnp.mean(raw * raw, axis=-1, keepdims=True)
        out_ref[head] = (raw * lax.rsqrt(mean + EPS) * gain_ref[...]).astype(out_ref.dtype)


def attend_kernel(
    image_start_ref,
    slot_image_ref,
    place_ref,
    q_ref,
    *refs,
    scale,
    group,
    slots_here,
):
    kv_refs = refs[:-5]
    out_ref, keys_ref, values_ref, begin_ref, total_ref = refs[-5:]
    slots, tile_rows, _ = keys_ref.shape
    ranks = slots // slots_here
    heads, tokens, head_dim = q_ref.shape
    members, own, _ = out_ref.shape
    n_images = image_start_ref.shape[0]
    plane_rank = place_ref[0]
    member = place_ref[1]
    first_token = plane_rank * tokens
    total_tokens = (slots // slots_here) * tokens
    limit = first_token + tokens
    ones = jnp.ones((tile_rows, head_dim), jnp.bfloat16)

    def take_from(kv_ref, at, rank, here, kept):
        slot = (rank * PLANE + member) * slots_here + here
        image = slot_image_ref[slot]
        start = image_start_ref[jnp.minimum(image, n_images - 1)]
        begin = jnp.where(image < n_images, start, total_tokens)
        rows = slice(here * tile_rows, (here + 1) * tile_rows)

        @pl.when(begin < limit)
        def _():
            keys_ref[kept] = kv_ref[at, rows, :head_dim]
            values_ref[kept] = jnp.concatenate([kv_ref[at, rows, head_dim:], ones], axis=1)
            begin_ref[kept] = begin

        return kept + (begin < limit).astype(jnp.int32)

    kept = jnp.int32(0)
    for kv_ref, offsets in zip(kv_refs, OFFSETS):
        for at, offset in enumerate(offsets):
            rank = lax.rem(plane_rank + offset + ranks, ranks)
            for here in range(slots_here):
                kept = take_from(kv_ref, at, rank, here, kept)
    turns = (kept + group - 1) // group

    def fill(place, _):
        keys_ref[place] = kv_refs[0][0, :tile_rows, :head_dim]
        values_ref[place] = jnp.concatenate([kv_refs[0][0, :tile_rows, head_dim:], ones], axis=1)
        begin_ref[place] = total_tokens
        return 0

    lax.fori_loop(kept, turns * group, fill, 0)
    total_ref[...] = jnp.zeros_like(total_ref)

    count = group * tile_rows
    lane = lax.broadcasted_iota(jnp.int32, (1, count), 1)
    position = first_token + lax.broadcasted_iota(jnp.int32, (tokens, 1), 0)

    def turn(number, _):
        base = number * group
        row_begin = jnp.zeros((1, count), jnp.int32)
        for place in range(group):
            row_begin = jnp.where(lane >= place * tile_rows, begin_ref[base + place], row_begin)
        keys = keys_ref[pl.ds(base, group)].reshape(count, head_dim)
        values = values_ref[pl.ds(base, group)].reshape(count, 2 * head_dim)
        visible = row_begin <= position

        def one_head(head, _):
            scores = lax.dot_general(
                q_ref[head],
                keys,
                (((1,), (1,)), ((), ())),
                preferred_element_type=jnp.float32,
            )
            weights = jnp.where(visible, jnp.exp2(scores * scale), 0.0)
            total_ref[head] += jnp.dot(
                weights.astype(jnp.bfloat16), values, preferred_element_type=jnp.float32
            )
            return 0

        lax.fori_loop(0, heads, one_head, 0)
        return 0

    lax.fori_loop(0, turns, turn, 0)

    column = lax.broadcasted_iota(jnp.int32, (own, head_dim), 1)
    for to in range(members):
        rows = slice(to * own, (to + 1) * own)
        sums = jnp.zeros((own, head_dim), jnp.float32)
        for head in range(heads):
            columns = slice(head * head_dim, (head + 1) * head_dim)
            out_ref[to, :, columns] = total_ref[head, rows, :head_dim].astype(out_ref.dtype)
            denom = total_ref[head, rows, head_dim:]
            high = denom.astype(jnp.bfloat16).astype(jnp.float32)
            sums = jnp.where(column == head, high, sums)
            sums = jnp.where(column == heads + head, denom - high, sums)
        out_ref[to, :, heads * head_dim :] = sums.astype(out_ref.dtype)


def combine_kernel(image_start_ref, place_ref, gate_ref, parts_ref, out_ref):
    members, own, width = parts_ref.shape
    plane_rank = place_ref[0]
    member = place_ref[1]
    out_width = out_ref.shape[1]
    head_dim = width - out_width
    heads = out_width // head_dim
    first = (plane_rank * members + member) * own
    position = first + lax.broadcasted_iota(jnp.int32, (own, 1), 0)
    seen = position >= image_start_ref[0]
    factor = jnp.tanh(gate_ref[...])
    sums = jnp.sum(parts_ref[:, :, out_width:].astype(jnp.float32), axis=0)
    for head in range(heads):
        columns = slice(head * head_dim, (head + 1) * head_dim)
        denom = sums[:, head : head + 1] + sums[:, heads + head : heads + head + 1]
        safe = jnp.where(seen, denom, 1.0)
        numer = jnp.sum(parts_ref[:, :, columns].astype(jnp.float32), axis=0)
        out_ref[:, columns] = jnp.where(seen, factor * numer / safe, 0.0).astype(out_ref.dtype)


def gather_along_z(block):
    ctx_size = lax.axis_size("ctx")

    def shift(value, distance):
        moved = distance * PLANE
        return lax.ppermute(
            value, "ctx", [(i, (i + moved) % ctx_size) for i in range(ctx_size)]
        )

    block = block[None]
    own = jnp.concatenate([shift(block, 4), block, shift(block, -4), shift(block, 8)])
    above, below = shift(own, 1), shift(own, -1)
    return own, above, below, shift(above[:2], 1), shift(below[1:3], -1)


def local(
    queries,
    q_gain,
    k_gain,
    attn_gate,
    vision,
    key_projection_matrix,
    value_projection_matrix,
    image_start,
    slot_image,
):
    ctx_size = lax.axis_size("ctx")
    head_size = lax.axis_size("head")
    ranks = ctx_size // PLANE
    own_index = lax.axis_index("ctx")
    plane_rank = own_index // PLANE
    member = own_index % PLANE
    place = jnp.stack([plane_rank, member]).astype(jnp.int32)
    head_dim = q_gain.shape[0]
    tokens, q_cols = queries.shape
    heads = q_cols // head_dim
    rows, features = vision.shape
    piece_rows, kv_cols = key_projection_matrix.shape
    in_plane = [[rank * PLANE + m for m in range(PLANE)] for rank in range(ranks)]
    whole_plane = [
        [rank * PLANE * head_size + i for i in range(PLANE * head_size)] for rank in range(ranks)
    ]

    with jax.named_scope("gather_queries"):
        all_queries = lax.all_gather(
            queries, "ctx", axis_index_groups=in_plane, axis=0, tiled=True
        )

    with jax.named_scope("spread_vision"):
        blocks = features // (piece_rows * PLANE)
        mine = pl.pallas_call(
            spread_kernel,
            out_shape=jax.ShapeDtypeStruct(
                (PLANE, head_size, blocks, rows, piece_rows), jnp.bfloat16
            ),
            in_specs=[vmem()],
            out_specs=vmem(),
            compiler_params=params(),
        )(vision)
        mine = mine.reshape(PLANE * head_size, blocks, rows, piece_rows)
        spread = lax.all_to_all(mine, ("ctx", "head"), 0, 0, axis_index_groups=whole_plane)
        spread = spread.reshape(PLANE, head_size, blocks, rows, piece_rows)

    with jax.named_scope("gather_projections"):
        weights = gather_along_z(
            jnp.concatenate([key_projection_matrix, value_projection_matrix], axis=1)
        )

    with jax.named_scope("norm_queries"):
        normed = pl.pallas_call(
            query_kernel,
            out_shape=jax.ShapeDtypeStruct((heads, PLANE * tokens, head_dim), jnp.bfloat16),
            in_specs=[vmem(), vmem()],
            out_specs=vmem(),
            compiler_params=params(),
        )(all_queries, q_gain.reshape(1, head_dim))
        spread, normed = lax.optimization_barrier((spread, normed))

    with jax.named_scope("project"):
        partial = pl.pallas_call(
            project_kernel,
            out_shape=jax.ShapeDtypeStruct((PLANE, rows, 3 * kv_cols), jnp.bfloat16),
            in_specs=[smem()] + [vmem()] * (1 + len(weights)),
            out_specs=vmem(),
            scratch_shapes=[pltpu.VMEM((ranks, piece_rows, 2 * kv_cols), jnp.bfloat16)],
            compiler_params=params(),
        )(place, spread, *weights)

    with jax.named_scope("sum_projections"):
        partial = lax.all_to_all(partial, "ctx", 0, 0, axis_index_groups=in_plane)
        own_kv = pl.pallas_call(
            finish_kernel,
            out_shape=jax.ShapeDtypeStruct((rows, 2 * kv_cols), jnp.bfloat16),
            in_specs=[vmem(), vmem()],
            out_specs=vmem(),
            compiler_params=params(),
        )(partial, k_gain.reshape(1, head_dim))

    with jax.named_scope("gather_keys_values"):
        all_kv = gather_along_z(own_kv)

    with jax.named_scope("attend"):
        slots_here = slot_image.shape[0] // ctx_size
        tile_rows = rows // slots_here
        slots = ranks * slots_here
        group = math.gcd(slots, 8)
        packed = pl.pallas_call(
            functools.partial(
                attend_kernel,
                scale=head_dim ** (-0.5) * math.log2(math.e),
                group=group,
                slots_here=slots_here,
            ),
            out_shape=jax.ShapeDtypeStruct((PLANE, tokens, q_cols + head_dim), jnp.bfloat16),
            in_specs=[smem()] * 3 + [vmem()] * (1 + len(all_kv)),
            out_specs=vmem(),
            scratch_shapes=[
                pltpu.VMEM((slots, tile_rows, head_dim), jnp.bfloat16),
                pltpu.VMEM((slots, tile_rows, 2 * head_dim), jnp.bfloat16),
                pltpu.SMEM((slots,), jnp.int32),
                pltpu.VMEM((heads, PLANE * tokens, 2 * head_dim), jnp.float32),
            ],
            compiler_params=params(),
        )(
            image_start,
            slot_image,
            place,
            normed,
            *all_kv,
        )

    with jax.named_scope("sum_attention"):
        packed = lax.all_to_all(packed, "ctx", 0, 0, axis_index_groups=in_plane)
        return pl.pallas_call(
            combine_kernel,
            out_shape=jax.ShapeDtypeStruct((tokens, q_cols), jnp.bfloat16),
            in_specs=[smem(), smem(), vmem(), vmem()],
            out_specs=vmem(),
            compiler_params=params(),
        )(image_start, place, attn_gate.reshape(1, 1), packed)


def solution(mesh):
    in_specs = (
        P("ctx", "head"),
        P(),
        P(),
        P(),
        P("ctx", "head"),
        P("ctx", "head"),
        P("ctx", "head"),
        P(),
        P(),
    )
    out_specs = P("ctx", "head")
    return jax.shard_map(local, mesh=mesh, in_specs=in_specs, out_specs=out_specs, check_vma=False)
```

```python
import functools
import math

import jax
import jax.numpy as jnp
from jax import lax
from jax.experimental import pallas as pl
from jax.experimental.pallas import tpu as pltpu
from jax.sharding import PartitionSpec as P

EPS = 1e-05
PLANE = 4
VMEM_LIMIT = 16 * 1024 * 1024
HIDE = -30000.0
STRIDE = 4
SOURCES = ((0, (0, 1, 2, 3)), (-1, (0, 1, 2, 3)), (1, (0, 1, 2, 3)), (2, (0, 1)), (2, (2, 3)))


def source_rank(plane_rank, step, turn):
    return lax.rem(plane_rank + step + STRIDE, STRIDE) + STRIDE * turn


def params(**more):
    return pltpu.CompilerParams(vmem_limit_bytes=VMEM_LIMIT, **more)


def vmem():
    return pl.BlockSpec(memory_space=pltpu.VMEM)


def smem():
    return pl.BlockSpec(memory_space=pltpu.SMEM)


def spread_kernel(x_ref, out_ref):
    members, peers, blocks, _, width = out_ref.shape
    for member in range(members):
        for block in range(blocks):
            first = (block * members + member) * width
            piece = x_ref[:, first : first + width]
            for peer in range(peers):
                out_ref[member, peer, block] = piece


def project_kernel(place_ref, x_ref, *refs):
    weight_refs, out_ref, all_ref = refs[:-2], refs[-2], refs[-1]
    _, depth, width = all_ref.shape
    members, peers, blocks, rows, _ = x_ref.shape
    head_dim = width // 2
    for ref, (step, several) in zip(weight_refs, SOURCES):
        for at, turn in enumerate(several):
            all_ref[source_rank(place_ref[0], step, turn)] = ref[at]
    total = None
    for peer in range(peers):
        for block in range(blocks):
            part = jnp.dot(
                x_ref[:, peer, block].reshape(members * rows, depth),
                all_ref[peer * blocks + block],
                preferred_element_type=jnp.float32,
            )
            total = part if total is None else total + part
    keys = total[:, :head_dim]
    high = keys.astype(jnp.bfloat16)
    low = (keys - high.astype(jnp.float32)).astype(jnp.bfloat16)
    values = total[:, head_dim:].astype(jnp.bfloat16)
    out_ref[...] = jnp.concatenate([high, low, values], axis=1).reshape(out_ref.shape)


def finish_kernel(parts_ref, gain_ref, out_ref):
    raw = jnp.sum(parts_ref[...].astype(jnp.float32), axis=0)
    head_dim = gain_ref.shape[1]
    keys = raw[:, :head_dim] + raw[:, head_dim : 2 * head_dim]
    mean = jnp.mean(keys * keys, axis=-1, keepdims=True)
    keys = keys * lax.rsqrt(mean + EPS) * gain_ref[...]
    out_ref[...] = jnp.concatenate([keys, raw[:, 2 * head_dim :]], axis=1).astype(out_ref.dtype)


def order_of(member):
    return member, member ^ 2, member ^ 1, member ^ 3


def query_kernel(place_ref, q_ref, gain_ref, out_ref):
    heads, all_tokens, head_dim = out_ref.shape
    tokens = all_tokens // PLANE
    for at, member in enumerate(order_of(place_ref[1])):
        rows = pl.ds(pl.multiple_of(member * tokens, tokens), tokens)
        for head in range(heads):
            raw = q_ref[rows, head * head_dim : (head + 1) * head_dim].astype(jnp.float32)
            mean = jnp.mean(raw * raw, axis=-1, keepdims=True)
            out_ref[head, at * tokens : (at + 1) * tokens] = (
                raw * lax.rsqrt(mean + EPS) * gain_ref[...]
            ).astype(out_ref.dtype)


def split_sums(sums, heads):
    column = lax.broadcasted_iota(jnp.int32, sums.shape, 1)
    high = sums.astype(jnp.bfloat16).astype(jnp.float32)
    low = pltpu.roll(sums - high, heads, 1)
    return jnp.where(column < heads, high, jnp.where(column < 2 * heads, low, 0.0))


def join_sums(parts, heads):
    return parts + pltpu.roll(parts, parts.shape[1] - heads, 1)


def attend_kernel(
    image_start_ref,
    slot_image_ref,
    place_ref,
    q_ref,
    *refs,
    scale,
    group,
    slots_here,
):
    kv_refs = refs[:-7]
    out_refs = refs[-7:-4]
    keys_ref, values_ref, late_ref, sums_ref = refs[-4:]
    slots, tile_rows, _ = keys_ref.shape
    ranks = slots // slots_here
    heads, tokens, head_dim = q_ref.shape
    own = tokens // PLANE
    n_images = image_start_ref.shape[0]
    plane_rank = place_ref[0]
    member = place_ref[1]
    first_token = plane_rank * tokens
    limit = first_token + tokens

    lane = lax.broadcasted_iota(jnp.int32, (own, head_dim), 1)
    starts = jnp.full((own, head_dim), ranks * tokens, jnp.int32)
    for image in range(n_images):
        starts = jnp.where(lane == image, image_start_ref[image], starts)
    for at, one in enumerate(order_of(member)):
        position = (
            first_token + one * own + lax.broadcasted_iota(jnp.int32, (own, head_dim), 0)
        )
        late_ref[at * own : (at + 1) * own] = jnp.where(starts > position, 1.0, 0.0).astype(
            jnp.bfloat16
        )

    tile_lane = lax.broadcasted_iota(jnp.int32, (tile_rows, head_dim), 1)
    ones = jnp.ones((tile_rows, head_dim), jnp.bfloat16)

    def put(kept, kv_ref, at, here, image):
        rows = slice(here * tile_rows, (here + 1) * tile_rows)
        mark = jnp.where(tile_lane == image, HIDE, 0.0).astype(jnp.bfloat16)
        keys_ref[kept] = jnp.concatenate([kv_ref[at, rows, :head_dim], mark], axis=1)
        values_ref[kept] = jnp.concatenate([kv_ref[at, rows, head_dim:], ones], axis=1)

    kept = jnp.int32(0)
    for kv_ref, (step, several) in zip(kv_refs, SOURCES):
        for at, turn in enumerate(several):
            rank = source_rank(plane_rank, step, turn)
            for here in range(slots_here):
                image = slot_image_ref[(rank * PLANE + member) * slots_here + here]
                start = image_start_ref[jnp.minimum(image, n_images - 1)]
                seen = jnp.logical_and(image < n_images, start < limit)
                pl.when(seen)(functools.partial(put, kept, kv_ref, at, here, image))
                kept = kept + seen.astype(jnp.int32)
    turns = (kept + group - 1) // group

    def fill(at, _):
        put(at, kv_refs[0], 0, 0, n_images)
        return 0

    lax.fori_loop(kept, turns * group, fill, 0)
    sums_ref[...] = jnp.zeros_like(sums_ref)
    column = lax.broadcasted_iota(jnp.int32, (tokens, head_dim), 1)

    def one_head(head, _, count):
        keys = keys_ref[:count].reshape(count * tile_rows, 2 * head_dim)
        values = values_ref[:count].reshape(count * tile_rows, 2 * head_dim)
        scores = lax.dot_general(
            jnp.concatenate([q_ref[head], late_ref[...]], axis=1),
            keys,
            (((1,), (1,)), ((), ())),
            preferred_element_type=jnp.float32,
        )
        weights = jnp.exp2(scores * scale).astype(jnp.bfloat16)
        total = jnp.dot(weights, values, preferred_element_type=jnp.float32)
        numer = total[:, :head_dim].astype(jnp.bfloat16)
        at = pl.ds(pl.multiple_of(head * head_dim, head_dim), head_dim)
        out_refs[0][:, at] = numer[:own]
        out_refs[1][:, at] = numer[own : 2 * own]
        out_refs[2][:, at] = numer[2 * own :]
        sums_ref[...] = jnp.where(column == head, total[:, head_dim:], sums_ref[...])
        return 0

    for turn in range(1, slots // group + 1):

        @pl.when(turns == turn)
        def _():
            lax.fori_loop(
                0, heads, functools.partial(one_head, count=turn * group), 0, unroll=2
            )

    @pl.when(turns == 0)
    def _():
        for out_ref in out_refs:
            out_ref[...] = jnp.zeros_like(out_ref)

    sums = split_sums(sums_ref[...], heads).astype(jnp.bfloat16)
    out_refs[0][:, heads * head_dim :] = sums[:own]
    out_refs[1][:, heads * head_dim :] = sums[own : 2 * own]
    out_refs[2][:, heads * head_dim :] = sums[2 * own :]


def add_kernel(kept_ref, came_ref, out_ref, *, heads):
    own, width = kept_ref.shape
    cut = width - 128
    for first in range(0, cut, 256):
        columns = slice(first, min(first + 256, cut))
        out_ref[:, columns] = (
            kept_ref[:, columns].astype(jnp.float32)
            + came_ref[own:, columns].astype(jnp.float32)
        ).astype(out_ref.dtype)
    sums = kept_ref[:, cut:].astype(jnp.float32) + came_ref[own:, cut:].astype(jnp.float32)
    out_ref[:, cut:] = split_sums(join_sums(sums, heads), heads).astype(out_ref.dtype)


def combine_kernel(image_start_ref, place_ref, gate_ref, kept_ref, core_ref, chip_ref, out_ref):
    own, width = kept_ref.shape
    out_width = out_ref.shape[1]
    head_dim = width - out_width
    heads = out_width // head_dim
    first = (place_ref[0] * PLANE + place_ref[1]) * own
    position = first + lax.broadcasted_iota(jnp.int32, (own, 1), 0)
    seen = position >= image_start_ref[0]
    factor = jnp.tanh(gate_ref[...])

    def total(columns):
        return (
            kept_ref[:, columns].astype(jnp.float32)
            + core_ref[:own, columns].astype(jnp.float32)
            + chip_ref[:, columns].astype(jnp.float32)
        )

    sums = join_sums(total(slice(out_width, width)), heads)
    for head in range(heads):
        columns = slice(head * head_dim, (head + 1) * head_dim)
        safe = jnp.where(seen, sums[:, head : head + 1], 1.0)
        out_ref[:, columns] = jnp.where(seen, total(columns) * (factor / safe), 0.0).astype(
            out_ref.dtype
        )


def gather_along_z(block):
    ctx_size = lax.axis_size("ctx")
    ranks = ctx_size // PLANE

    def shift(value, distance):
        moved = distance * PLANE
        return lax.ppermute(
            value, "ctx", [(i, (i + moved) % ctx_size) for i in range(ctx_size)]
        )

    groups = [
        [rank * PLANE + member for rank in range(first, ranks, STRIDE)]
        for member in range(PLANE)
        for first in range(STRIDE)
    ]
    own = lax.all_gather(block, "ctx", axis_index_groups=groups)
    half = own.shape[0] // 2
    return own, shift(own, 1), shift(own, -1), shift(own[:half], 2), shift(own[half:], -2)


def other_member(value, mask):
    ctx_size = lax.axis_size("ctx")
    return lax.ppermute(value, "ctx", [(i, i ^ mask) for i in range(ctx_size)])


def local(
    queries,
    q_gain,
    k_gain,
    attn_gate,
    vision,
    key_projection_matrix,
    value_projection_matrix,
    image_start,
    slot_image,
):
    ctx_size = lax.axis_size("ctx")
    head_size = lax.axis_size("head")
    ranks = ctx_size // PLANE
    own_index = lax.axis_index("ctx")
    plane_rank = own_index // PLANE
    member = own_index % PLANE
    place = jnp.stack([plane_rank, member]).astype(jnp.int32)
    head_dim = q_gain.shape[0]
    tokens, q_cols = queries.shape
    heads = q_cols // head_dim
    rows, features = vision.shape
    piece_rows, kv_cols = key_projection_matrix.shape
    in_plane = [[rank * PLANE + m for m in range(PLANE)] for rank in range(ranks)]
    whole_plane = [
        [rank * PLANE * head_size + i for i in range(PLANE * head_size)] for rank in range(ranks)
    ]

    with jax.named_scope("gather_queries"):
        all_queries = lax.all_gather(
            queries, "ctx", axis_index_groups=in_plane, axis=0, tiled=True
        )

    with jax.named_scope("spread_vision"):
        blocks = features // (piece_rows * PLANE)
        mine = pl.pallas_call(
            spread_kernel,
            out_shape=jax.ShapeDtypeStruct(
                (PLANE, head_size, blocks, rows, piece_rows), jnp.bfloat16
            ),
            in_specs=[vmem()],
            out_specs=vmem(),
            compiler_params=params(),
        )(vision)
        mine = mine.reshape(PLANE * head_size, blocks, rows, piece_rows)
        spread = lax.all_to_all(mine, ("ctx", "head"), 0, 0, axis_index_groups=whole_plane)
        spread = spread.reshape(PLANE, head_size, blocks, rows, piece_rows)

    with jax.named_scope("gather_projections"):
        weights = gather_along_z(
            jnp.concatenate([key_projection_matrix, value_projection_matrix], axis=1)
        )

    with jax.named_scope("norm_queries"):
        normed = pl.pallas_call(
            query_kernel,
            out_shape=jax.ShapeDtypeStruct((heads, PLANE * tokens, head_dim), jnp.bfloat16),
            in_specs=[smem(), vmem(), vmem()],
            out_specs=vmem(),
            compiler_params=params(),
        )(place, all_queries, q_gain.reshape(1, head_dim))
        spread, normed = lax.optimization_barrier((spread, normed))

    with jax.named_scope("project"):
        partial = pl.pallas_call(
            project_kernel,
            out_shape=jax.ShapeDtypeStruct((PLANE, rows, 3 * kv_cols), jnp.bfloat16),
            in_specs=[smem()] + [vmem()] * (1 + len(weights)),
            out_specs=vmem(),
            scratch_shapes=[pltpu.VMEM((ranks, piece_rows, 2 * kv_cols), jnp.bfloat16)],
            compiler_params=params(),
        )(place, spread, *weights)

    with jax.named_scope("sum_projections"):
        partial = lax.all_to_all(partial, "ctx", 0, 0, axis_index_groups=in_plane)
        own_kv = pl.pallas_call(
            finish_kernel,
            out_shape=jax.ShapeDtypeStruct((rows, 2 * kv_cols), jnp.bfloat16),
            in_specs=[vmem(), vmem()],
            out_specs=vmem(),
            compiler_params=params(),
        )(partial, k_gain.reshape(1, head_dim))

    with jax.named_scope("gather_keys_values"):
        all_kv = gather_along_z(own_kv)

    with jax.named_scope("attend"):
        slots_here = slot_image.shape[0] // ctx_size
        tile_rows = rows // slots_here
        slots = ranks * slots_here
        width = q_cols + head_dim
        shapes = [(tokens, width), (tokens, width), (2 * tokens, width)]
        kept, to_chip, to_core = pl.pallas_call(
            functools.partial(
                attend_kernel,
                scale=head_dim ** (-0.5) * math.log2(math.e),
                group=math.gcd(slots, 4),
                slots_here=slots_here,
            ),
            out_shape=[jax.ShapeDtypeStruct(shape, jnp.bfloat16) for shape in shapes],
            in_specs=[smem()] * 3 + [vmem()] * (1 + len(all_kv)),
            out_specs=[vmem()] * 3,
            scratch_shapes=[
                pltpu.VMEM((slots, tile_rows, 2 * head_dim), jnp.bfloat16),
                pltpu.VMEM((slots, tile_rows, 2 * head_dim), jnp.bfloat16),
                pltpu.VMEM((PLANE * tokens, head_dim), jnp.bfloat16),
                pltpu.VMEM((PLANE * tokens, head_dim), jnp.float32),
            ],
            compiler_params=params(),
        )(image_start, slot_image, place, normed, *all_kv)

    with jax.named_scope("sum_attention"):
        from_core = other_member(to_core, 1)
        to_chip = pl.pallas_call(
            functools.partial(add_kernel, heads=heads),
            out_shape=jax.ShapeDtypeStruct((tokens, width), jnp.bfloat16),
            in_specs=[vmem(), vmem()],
            out_specs=vmem(),
            compiler_params=params(),
        )(to_chip, from_core)
        from_chip = other_member(to_chip, 2)
        return pl.pallas_call(
            combine_kernel,
            out_shape=jax.ShapeDtypeStruct((tokens, q_cols), jnp.bfloat16),
            in_specs=[smem(), smem()] + [vmem()] * 4,
            out_specs=vmem(),
            compiler_params=params(),
        )(image_start, place, attn_gate.reshape(1, 1), kept, from_core, from_chip)


def solution(mesh):
    in_specs = (
        P("ctx", "head"),
        P(),
        P(),
        P(),
        P("ctx", "head"),
        P("ctx", "head"),
        P("ctx", "head"),
        P(),
        P(),
    )
    out_specs = P("ctx", "head")
    return jax.shard_map(local, mesh=mesh, in_specs=in_specs, out_specs=out_specs, check_vma=False)
```

```python
import functools
import math

import jax
import jax.numpy as jnp
from jax import lax
from jax.experimental import pallas as pl
from jax.experimental.pallas import tpu as pltpu
from jax.sharding import PartitionSpec as P

EPS = 1e-05
PLANE = 4
VMEM_LIMIT = 16 * 1024 * 1024
SPREAD_LIMIT = 62 * 1024 * 1024
HIDE = -30000.0
STRIDE = 4
SOURCES = ((0, (0, 1, 2, 3)), (-1, (0, 1, 2, 3)), (1, (0, 1, 2, 3)), (2, (0, 1)), (2, (2, 3)))

FIRST = 3


def source_rank(plane_rank, step, turn):
    return lax.rem(plane_rank + step + STRIDE, STRIDE) + STRIDE * turn


def params(**more):
    return pltpu.CompilerParams(vmem_limit_bytes=VMEM_LIMIT, **more)


def vmem():
    return pl.BlockSpec(memory_space=pltpu.VMEM)


def smem():
    return pl.BlockSpec(memory_space=pltpu.SMEM)


def spread_kernel(x_ref, out_ref, pieces_ref, sems):
    members, peers, blocks, _, width = out_ref.shape
    copies = []
    for member in range(members):
        for block in range(blocks):
            first = (block * members + member) * width
            pieces_ref[member, block] = x_ref[:, first : first + width]
        for peer in range(peers):
            copies.append(
                pltpu.make_async_copy(
                    pieces_ref.at[member], out_ref.at[member, peer], sems.at[len(copies)]
                )
            )
            copies[-1].start()
    for copy in copies:
        copy.wait()


def order_of(member):
    return member, member ^ 2, member ^ 1, member ^ 3


def products(place_ref, x_ref, weight_refs, sources):
    depth = x_ref.shape[3]
    total = None
    for ref, (step, several) in zip(weight_refs, sources):
        for at in range(0, len(several), 2):
            both = [source_rank(place_ref[0], step, several[at + i]) for i in range(2)]
            part = jnp.dot(
                jnp.concatenate(
                    [
                        jnp.concatenate([x_ref[member, rank] for rank in both], axis=1)
                        for member in order_of(place_ref[1])
                    ],
                    axis=0,
                ),
                ref[at : at + 2].reshape(2 * depth, ref.shape[2]),
                preferred_element_type=jnp.float32,
            )
            total = part if total is None else total + part
    return total


def project_first_kernel(place_ref, x_ref, *refs):
    refs[-1][...] = products(place_ref, x_ref, refs[:-1], SOURCES[:FIRST])


def pack_products(total):
    head_dim = total.shape[1] // 2
    keys = total[:, :head_dim]
    high = keys.astype(jnp.bfloat16)
    low = (keys - high.astype(jnp.float32)).astype(jnp.bfloat16)
    return jnp.concatenate([high, low, total[:, head_dim:].astype(jnp.bfloat16)], axis=1)


def unpack_products(parts):
    head_dim = parts.shape[1] // 3
    parts = parts.astype(jnp.float32)
    keys = parts[:, :head_dim] + parts[:, head_dim : 2 * head_dim]
    return jnp.concatenate([keys, parts[:, 2 * head_dim :]], axis=1)


def project_last_kernel(place_ref, x_ref, *refs):
    weight_refs, first_ref, out_refs = refs[:-4], refs[-4], refs[-3:]
    total = first_ref[...] + products(place_ref, x_ref, weight_refs, SOURCES[FIRST:])
    packed = pack_products(total)
    rows = x_ref.shape[2]
    for out_ref, (start, stop) in zip(out_refs, ((0, 1), (1, 2), (2, 4))):
        out_ref[...] = packed[start * rows : stop * rows]


def add_products_kernel(kept_ref, came_ref, out_ref):
    rows = kept_ref.shape[0]
    out_ref[...] = pack_products(
        unpack_products(kept_ref[...]) + unpack_products(came_ref[rows:])
    )


def finish_kernel(kept_ref, core_ref, chip_ref, gain_ref, out_ref):
    rows = kept_ref.shape[0]
    raw = (
        unpack_products(kept_ref[...])
        + unpack_products(core_ref[:rows])
        + unpack_products(chip_ref[...])
    )
    head_dim = gain_ref.shape[1]
    keys = raw[:, :head_dim]
    mean = jnp.mean(keys * keys, axis=-1, keepdims=True)
    keys = keys * lax.rsqrt(mean + EPS) * gain_ref[...]
    out_ref[...] = jnp.concatenate([keys, raw[:, head_dim:]], axis=1).astype(out_ref.dtype)


def query_kernel(q_ref, gain_ref, out_ref):
    heads, _, head_dim = out_ref.shape
    for head in range(heads):
        raw = q_ref[:, head * head_dim : (head + 1) * head_dim].astype(jnp.float32)
        mean = jnp.mean(raw * raw, axis=-1, keepdims=True)
        out_ref[head] = (raw * lax.rsqrt(mean + EPS) * gain_ref[...]).astype(out_ref.dtype)


def split_sums(sums, heads):
    column = lax.broadcasted_iota(jnp.int32, sums.shape, 1)
    high = sums.astype(jnp.bfloat16).astype(jnp.float32)
    low = pltpu.roll(sums - high, heads, 1)
    return jnp.where(column < heads, high, jnp.where(column < 2 * heads, low, 0.0))


def join_sums(parts, heads):
    return parts + pltpu.roll(parts, parts.shape[1] - heads, 1)


def prepare_kernel(
    image_start_ref, slot_image_ref, place_ref, *refs, tokens, group, slots_here
):
    kv_refs = refs[:-4]
    keys_ref, values_ref, late_ref, turns_ref = refs[-4:]
    slots, tile_rows, width = keys_ref.shape
    head_dim = width // 2
    ranks = slots // slots_here
    n_images = image_start_ref.shape[0]
    own = tokens // PLANE
    plane_rank = place_ref[0]
    member = place_ref[1]
    first_token = plane_rank * tokens
    limit = first_token + tokens

    lane = lax.broadcasted_iota(jnp.int32, (own, head_dim), 1)
    starts = jnp.full((own, head_dim), ranks * tokens, jnp.int32)
    for image in range(n_images):
        starts = jnp.where(lane == image, image_start_ref[image], starts)
    for at, one in enumerate(order_of(member)):
        position = (
            first_token + one * own + lax.broadcasted_iota(jnp.int32, (own, head_dim), 0)
        )
        late_ref[at * own : (at + 1) * own] = jnp.where(starts > position, 1.0, 0.0).astype(
            jnp.bfloat16
        )

    tile_lane = lax.broadcasted_iota(jnp.int32, (tile_rows, head_dim), 1)
    ones = jnp.ones((tile_rows, head_dim), jnp.bfloat16)

    def put(kept, kv_ref, at, here, image):
        rows = slice(here * tile_rows, (here + 1) * tile_rows)
        mark = jnp.where(tile_lane == image, HIDE, 0.0).astype(jnp.bfloat16)
        keys_ref[kept] = jnp.concatenate([kv_ref[at, rows, :head_dim], mark], axis=1)
        values_ref[kept] = jnp.concatenate([kv_ref[at, rows, head_dim:], ones], axis=1)

    kept = jnp.int32(0)
    for kv_ref, (step, several) in zip(kv_refs, SOURCES):
        for at, turn in enumerate(several):
            rank = source_rank(plane_rank, step, turn)
            for here in range(slots_here):
                image = slot_image_ref[(rank * PLANE + member) * slots_here + here]
                start = image_start_ref[jnp.minimum(image, n_images - 1)]
                seen = jnp.logical_and(image < n_images, start < limit)
                pl.when(seen)(functools.partial(put, kept, kv_ref, at, here, image))
                kept = kept + seen.astype(jnp.int32)
    turns = (kept + group - 1) // group
    turns_ref[0] = turns

    def fill(at, _):
        put(at, kv_refs[0], 0, 0, n_images)
        return 0

    lax.fori_loop(kept, turns * group, fill, 0)


def attend_kernel(turns_ref, late_ref, keys_ref, values_ref, *refs, scale, group, heads, first, halves):
    q_refs, out_ref, sums_ref = refs[:-2], refs[-2], refs[-1]
    slots, tile_rows, width = keys_ref.shape
    _, own, head_dim = q_refs[0].shape
    count = own * len(q_refs)
    rows = slice(first, first + count)
    sums_ref[...] = jnp.zeros_like(sums_ref)
    column = lax.broadcasted_iota(jnp.int32, (count, head_dim), 1)

    together = max(1, 512 // count)

    def some_heads(number, _, kept):
        keys = keys_ref[:kept].reshape(kept * tile_rows, width)
        values = values_ref[:kept].reshape(kept * tile_rows, width)
        several = [together * number + i for i in range(together)]
        late = late_ref[rows]
        scores = lax.dot_general(
            jnp.concatenate(
                [
                    jnp.concatenate(
                        [
                            jnp.concatenate(
                                [ref[half * heads + head] for ref, half in zip(q_refs, halves)],
                                axis=0,
                            ),
                            late,
                        ],
                        axis=1,
                    )
                    for head in several
                ],
                axis=0,
            ),
            keys,
            (((1,), (1,)), ((), ())),
            preferred_element_type=jnp.float32,
        )
        weights = jnp.exp2(scores * scale).astype(jnp.bfloat16)
        both = jnp.dot(weights, values, preferred_element_type=jnp.float32)
        sums = sums_ref[...]
        for i, head in enumerate(several):
            total = both[i * count : (i + 1) * count]
            at = pl.ds(pl.multiple_of(head * head_dim, head_dim), head_dim)
            out_ref[:, at] = total[:, :head_dim].astype(out_ref.dtype)
            sums = jnp.where(column == head, total[:, head_dim:], sums)
        sums_ref[...] = sums
        return 0

    turns = turns_ref[0]
    for turn in range(1, slots // group + 1):

        @pl.when(turns == turn)
        def _():
            lax.fori_loop(
                0, heads // together, functools.partial(some_heads, kept=turn * group), 0, unroll=2
            )

    @pl.when(turns == 0)
    def _():
        out_ref[...] = jnp.zeros_like(out_ref)

    out_ref[:, heads * head_dim :] = split_sums(sums_ref[...], heads).astype(out_ref.dtype)


def add_kernel(kept_ref, came_ref, out_ref, *, heads):
    own, width = kept_ref.shape
    cut = width - 128
    for first in range(0, cut, 256):
        columns = slice(first, min(first + 256, cut))
        out_ref[:, columns] = (
            kept_ref[:, columns].astype(jnp.float32)
            + came_ref[own:, columns].astype(jnp.float32)
        ).astype(out_ref.dtype)
    sums = kept_ref[:, cut:].astype(jnp.float32) + came_ref[own:, cut:].astype(jnp.float32)
    out_ref[:, cut:] = split_sums(join_sums(sums, heads), heads).astype(out_ref.dtype)


def combine_kernel(image_start_ref, place_ref, gate_ref, kept_ref, core_ref, chip_ref, out_ref):
    own, width = kept_ref.shape
    out_width = out_ref.shape[1]
    head_dim = width - out_width
    heads = out_width // head_dim
    first = (place_ref[0] * PLANE + place_ref[1]) * own
    position = first + lax.broadcasted_iota(jnp.int32, (own, 1), 0)
    seen = position >= image_start_ref[0]
    factor = jnp.tanh(gate_ref[...])

    def total(columns):
        return (
            kept_ref[:, columns].astype(jnp.float32)
            + core_ref[:own, columns].astype(jnp.float32)
            + chip_ref[:, columns].astype(jnp.float32)
        )

    sums = join_sums(total(slice(out_width, width)), heads)
    share = jnp.where(seen, factor / jnp.where(seen, sums, 1.0), 0.0)
    for head in range(heads):
        columns = slice(head * head_dim, (head + 1) * head_dim)
        out_ref[:, columns] = (total(columns) * share[:, head : head + 1]).astype(out_ref.dtype)


def gather_along_z(block, beside=None):
    ctx_size = lax.axis_size("ctx")
    ranks = ctx_size // PLANE

    def shift(value, distance):
        moved = distance * PLANE
        return lax.ppermute(
            value, "ctx", [(i, (i + moved) % ctx_size) for i in range(ctx_size)]
        )

    groups = [
        [rank * PLANE + member for rank in range(first, ranks, STRIDE)]
        for member in range(PLANE)
        for first in range(STRIDE)
    ]
    own = lax.all_gather(block, "ctx", axis_index_groups=groups)
    if beside is not None:
        own, beside = lax.optimization_barrier((own, beside))
    half = own.shape[0] // 2
    parts = own, shift(own, 1), shift(own, -1), shift(own[:half], 2), shift(own[half:], -2)
    return parts, beside


def other_member(value, mask):
    ctx_size = lax.axis_size("ctx")
    return lax.ppermute(value, "ctx", [(i, i ^ mask) for i in range(ctx_size)])


def local(
    queries,
    q_gain,
    k_gain,
    attn_gate,
    vision,
    key_projection_matrix,
    value_projection_matrix,
    image_start,
    slot_image,
):
    ctx_size = lax.axis_size("ctx")
    head_size = lax.axis_size("head")
    ranks = ctx_size // PLANE
    own_index = lax.axis_index("ctx")
    plane_rank = own_index // PLANE
    member = own_index % PLANE
    place = jnp.stack([plane_rank, member]).astype(jnp.int32)
    head_dim = q_gain.shape[0]
    tokens, q_cols = queries.shape
    heads = q_cols // head_dim
    rows, features = vision.shape
    piece_rows, kv_cols = key_projection_matrix.shape
    in_plane = [[rank * PLANE + m for m in range(PLANE)] for rank in range(ranks)]
    whole_plane = [
        [rank * PLANE * head_size + i for i in range(PLANE * head_size)] for rank in range(ranks)
    ]

    with jax.named_scope("norm_queries"):
        normed = pl.pallas_call(
            query_kernel,
            out_shape=jax.ShapeDtypeStruct((heads, tokens, head_dim), jnp.bfloat16),
            in_specs=[vmem(), vmem()],
            out_specs=vmem(),
            compiler_params=params(),
        )(queries, q_gain.reshape(1, head_dim))

    with jax.named_scope("spread_vision"):
        blocks = features // (piece_rows * PLANE)
        mine = pl.pallas_call(
            spread_kernel,
            out_shape=jax.ShapeDtypeStruct(
                (PLANE, head_size, blocks, rows, piece_rows), jnp.bfloat16
            ),
            in_specs=[vmem()],
            out_specs=pl.BlockSpec(memory_space=pltpu.HBM),
            scratch_shapes=[
                pltpu.VMEM((PLANE, blocks, rows, piece_rows), jnp.bfloat16),
                pltpu.SemaphoreType.DMA((PLANE * head_size,)),
            ],
            compiler_params=pltpu.CompilerParams(vmem_limit_bytes=SPREAD_LIMIT),
        )(vision)
        mine = mine.reshape(PLANE * head_size, blocks, rows, piece_rows)
        spread = lax.all_to_all(mine, ("ctx", "head"), 0, 0, axis_index_groups=whole_plane)
        spread = spread.reshape(PLANE, ranks, rows, piece_rows)

    with jax.named_scope("gather_projections"):
        weights, _ = gather_along_z(
            jnp.concatenate([key_projection_matrix, value_projection_matrix], axis=1)
        )

    with jax.named_scope("share_queries"):
        core_queries = other_member(normed, 1)
        spread, core_queries = lax.optimization_barrier((spread, core_queries))
        chip_queries = other_member(jnp.concatenate([normed, core_queries]), 2)

    with jax.named_scope("project"):
        partial = pl.pallas_call(
            project_first_kernel,
            out_shape=jax.ShapeDtypeStruct((PLANE * rows, 2 * kv_cols), jnp.float32),
            in_specs=[smem()] + [vmem()] * (1 + FIRST),
            out_specs=vmem(),
            compiler_params=params(),
        )(place, spread, *weights[:FIRST])
        triple = 3 * kv_cols
        shapes = [(rows, triple), (rows, triple), (2 * rows, triple)]
        kept, to_chip, to_core = pl.pallas_call(
            project_last_kernel,
            out_shape=[jax.ShapeDtypeStruct(shape, jnp.bfloat16) for shape in shapes],
            in_specs=[smem()] + [vmem()] * (2 + len(weights) - FIRST),
            out_specs=[vmem()] * 3,
            compiler_params=params(),
        )(place, spread, *weights[FIRST:], partial)

    with jax.named_scope("sum_projections"):
        from_core = other_member(to_core, 1)
        to_chip = pl.pallas_call(
            add_products_kernel,
            out_shape=jax.ShapeDtypeStruct((rows, triple), jnp.bfloat16),
            in_specs=[vmem()] * 2,
            out_specs=vmem(),
            compiler_params=params(),
        )(to_chip, from_core)
        from_chip = other_member(to_chip, 2)
        own_kv = pl.pallas_call(
            finish_kernel,
            out_shape=jax.ShapeDtypeStruct((rows, 2 * kv_cols), jnp.bfloat16),
            in_specs=[vmem()] * 4,
            out_specs=vmem(),
            compiler_params=params(),
        )(kept, from_core, from_chip, k_gain.reshape(1, head_dim))

    with jax.named_scope("gather_keys_values"):
        all_kv, chip_queries = gather_along_z(own_kv, chip_queries)

    with jax.named_scope("attend"):
        slots_here = slot_image.shape[0] // ctx_size
        tile_rows = rows // slots_here
        slots = ranks * slots_here
        group = math.gcd(slots, 4)
        width = q_cols + head_dim
        packed = (slots, tile_rows, 2 * head_dim)
        turns, late, keys, values = [
            jax.ShapeDtypeStruct((1,), jnp.int32),
            jax.ShapeDtypeStruct((PLANE * tokens, head_dim), jnp.bfloat16),
            jax.ShapeDtypeStruct(packed, jnp.bfloat16),
            jax.ShapeDtypeStruct(packed, jnp.bfloat16),
        ]
        keys, values, late, turns = pl.pallas_call(
            functools.partial(
                prepare_kernel, tokens=PLANE * tokens, group=group, slots_here=slots_here
            ),
            out_shape=[keys, values, late, turns],
            in_specs=[smem()] * 3 + [vmem()] * len(all_kv),
            out_specs=[vmem()] * 3 + [smem()],
            compiler_params=params(),
        )(image_start, slot_image, place, *all_kv)

        def attend(first, *sources):
            rows_here = len(sources) * tokens
            scores = heads * rows_here * slots * tile_rows
            return pl.pallas_call(
                functools.partial(
                    attend_kernel,
                    scale=head_dim ** (-0.5) * math.log2(math.e),
                    group=group,
                    heads=heads,
                    first=first * tokens,
                    halves=tuple(half for _, half in sources),
                ),
                out_shape=jax.ShapeDtypeStruct((rows_here, width), jnp.bfloat16),
                in_specs=[smem()] + [vmem()] * (3 + len(sources)),
                out_specs=vmem(),
                scratch_shapes=[pltpu.VMEM((rows_here, head_dim), jnp.float32)],
                compiler_params=params(),
                cost_estimate=pl.CostEstimate(
                    flops=8 * scores * head_dim,
                    bytes_accessed=4 * rows_here * width,
                    transcendentals=scores,
                ),
            )(turns, late, keys, values, *(source for source, _ in sources))

        to_core = attend(2, (core_queries, 0), (chip_queries, 1))
        from_core = other_member(to_core, 1)
        to_chip = attend(1, (chip_queries, 0))

    with jax.named_scope("sum_attention"):
        to_chip = pl.pallas_call(
            functools.partial(add_kernel, heads=heads),
            out_shape=jax.ShapeDtypeStruct((tokens, width), jnp.bfloat16),
            in_specs=[vmem(), vmem()],
            out_specs=vmem(),
            compiler_params=params(),
        )(to_chip, from_core)
        from_chip = other_member(to_chip, 2)
        kept = attend(0, (normed, 0))
        return pl.pallas_call(
            combine_kernel,
            out_shape=jax.ShapeDtypeStruct((tokens, q_cols), jnp.bfloat16),
            in_specs=[smem(), smem()] + [vmem()] * 4,
            out_specs=vmem(),
            compiler_params=params(),
        )(image_start, place, attn_gate.reshape(1, 1), kept, from_core, from_chip)


def solution(mesh):
    in_specs = (
        P("ctx", "head"),
        P(),
        P(),
        P(),
        P("ctx", "head"),
        P("ctx", "head"),
        P("ctx", "head"),
        P(),
        P(),
    )
    out_specs = P("ctx", "head")
    return jax.shard_map(local, mesh=mesh, in_specs=in_specs, out_specs=out_specs, check_vma=False)
```

```python
import functools
import math

import jax
import jax.numpy as jnp
from jax import lax
from jax.experimental import pallas as pl
from jax.experimental.pallas import tpu as pltpu
from jax.sharding import PartitionSpec as P

EPS = 1e-05
PLANE = 4
VMEM_LIMIT = 16 * 1024 * 1024
SPREAD_LIMIT = 62 * 1024 * 1024
HIDE = -30000.0
STRIDE = 4
SOURCES = ((0, (0, 1, 2, 3)), (-1, (0, 1, 2, 3)), (1, (0, 1, 2, 3)), (2, (0, 1, 2, 3)))

FIRST = 3


def source_rank(plane_rank, step, turn):
    return lax.rem(plane_rank + step + STRIDE, STRIDE) + STRIDE * turn


def params(**more):
    return pltpu.CompilerParams(vmem_limit_bytes=VMEM_LIMIT, **more)


def vmem():
    return pl.BlockSpec(memory_space=pltpu.VMEM)


def smem():
    return pl.BlockSpec(memory_space=pltpu.SMEM)


def spread_kernel(x_ref, out_ref, pieces_ref, sems):
    members, peers, blocks, _, width = out_ref.shape
    copies = []
    for member in range(members):
        for block in range(blocks):
            first = (block * members + member) * width
            pieces_ref[member, block] = x_ref[:, first : first + width]
        for peer in range(peers):
            copies.append(
                pltpu.make_async_copy(
                    pieces_ref.at[member], out_ref.at[member, peer], sems.at[len(copies)]
                )
            )
            copies[-1].start()
    for copy in copies:
        copy.wait()


def order_of(member):
    return member, member ^ 2, member ^ 1, member ^ 3


def products(place_ref, x_ref, weight_refs, sources):
    depth = x_ref.shape[3]
    total = None
    for ref, (step, several) in zip(weight_refs, sources):
        for at in range(0, len(several), 2):
            both = [source_rank(place_ref[0], step, several[at + i]) for i in range(2)]
            part = jnp.dot(
                jnp.concatenate(
                    [
                        jnp.concatenate([x_ref[member, rank] for rank in both], axis=1)
                        for member in order_of(place_ref[1])
                    ],
                    axis=0,
                ),
                ref[at : at + 2].reshape(2 * depth, ref.shape[2]),
                preferred_element_type=jnp.float32,
            )
            total = part if total is None else total + part
    return total


def project_first_kernel(place_ref, x_ref, *refs):
    refs[-1][...] = products(place_ref, x_ref, refs[:-1], SOURCES[:FIRST])


def pack_products(total):
    head_dim = total.shape[1] // 2
    keys = total[:, :head_dim]
    high = keys.astype(jnp.bfloat16)
    low = (keys - high.astype(jnp.float32)).astype(jnp.bfloat16)
    return jnp.concatenate([high, low, total[:, head_dim:].astype(jnp.bfloat16)], axis=1)


def unpack_products(parts):
    head_dim = parts.shape[1] // 3
    parts = parts.astype(jnp.float32)
    keys = parts[:, :head_dim] + parts[:, head_dim : 2 * head_dim]
    return jnp.concatenate([keys, parts[:, 2 * head_dim :]], axis=1)


def project_last_kernel(place_ref, x_ref, *refs):
    weight_refs, first_ref, out_refs = refs[:-4], refs[-4], refs[-3:]
    total = first_ref[...] + products(place_ref, x_ref, weight_refs, SOURCES[FIRST:])
    packed = pack_products(total)
    rows = x_ref.shape[2]
    for out_ref, (start, stop) in zip(out_refs, ((0, 1), (1, 2), (2, 4))):
        out_ref[...] = packed[start * rows : stop * rows]


def add_products_kernel(kept_ref, came_ref, out_ref):
    rows = kept_ref.shape[0]
    out_ref[...] = pack_products(
        unpack_products(kept_ref[...]) + unpack_products(came_ref[rows:])
    )


def finish_kernel(kept_ref, core_ref, chip_ref, gain_ref, out_ref):
    rows = kept_ref.shape[0]
    raw = (
        unpack_products(kept_ref[...])
        + unpack_products(core_ref[:rows])
        + unpack_products(chip_ref[...])
    )
    head_dim = gain_ref.shape[1]
    keys = raw[:, :head_dim]
    mean = jnp.mean(keys * keys, axis=-1, keepdims=True)
    keys = keys * lax.rsqrt(mean + EPS) * gain_ref[...]
    out_ref[...] = jnp.concatenate([keys, raw[:, head_dim:]], axis=1).astype(out_ref.dtype)


def query_kernel(q_ref, gain_ref, out_ref):
    heads, _, head_dim = out_ref.shape
    for head in range(heads):
        raw = q_ref[:, head * head_dim : (head + 1) * head_dim].astype(jnp.float32)
        mean = jnp.mean(raw * raw, axis=-1, keepdims=True)
        out_ref[head] = (raw * lax.rsqrt(mean + EPS) * gain_ref[...]).astype(out_ref.dtype)


def split_sums(sums, heads):
    column = lax.broadcasted_iota(jnp.int32, sums.shape, 1)
    high = sums.astype(jnp.bfloat16).astype(jnp.float32)
    low = pltpu.roll(sums - high, heads, 1)
    return jnp.where(column < heads, high, jnp.where(column < 2 * heads, low, 0.0))


def join_sums(parts, heads):
    return parts + pltpu.roll(parts, parts.shape[1] - heads, 1)


def put_slot(keys_ref, values_ref, to, kv_ref, at, here, image):
    _, tile_rows, width = keys_ref.shape
    head_dim = width // 2
    rows = slice(here * tile_rows, (here + 1) * tile_rows)
    lane = lax.broadcasted_iota(jnp.int32, (tile_rows, head_dim), 1)
    mark = jnp.where(lane == image, HIDE, 0.0).astype(jnp.bfloat16)
    ones = jnp.ones((tile_rows, head_dim), jnp.bfloat16)
    keys_ref[to] = jnp.concatenate([kv_ref[at, rows, :head_dim], mark], axis=1)
    values_ref[to] = jnp.concatenate([kv_ref[at, rows, head_dim:], ones], axis=1)


def weigh(q_refs, halves, heads, several, late, keys, values, scale):
    q = [
        jnp.concatenate(
            [
                jnp.concatenate(
                    [ref[half * heads + head] for ref, half in zip(q_refs, halves)], axis=0
                ),
                late,
            ],
            axis=1,
        )
        for head in several
    ]
    scores = lax.dot_general(
        jnp.concatenate(q, axis=0),
        keys,
        (((1,), (1,)), ((), ())),
        preferred_element_type=jnp.float32,
    )
    weights = jnp.exp2(scores * scale).astype(jnp.bfloat16)
    total = jnp.dot(weights, values, preferred_element_type=jnp.float32)
    rows = late.shape[0]
    return [total[i * rows : (i + 1) * rows] for i in range(len(several))]


def attend_first_kernel(
    image_start_ref, slot_image_ref, place_ref, *refs, scale, slots_here, heads, halves
):
    kv_ref, q_refs = refs[0], refs[1 : 1 + PLANE]
    numer_ref, sums_ref, late_ref, keys_ref, values_ref = refs[1 + PLANE :]
    _, own, head_dim = q_refs[0].shape
    n_images = image_start_ref.shape[0]
    tokens = PLANE * own
    plane_rank = place_ref[0]
    member = place_ref[1]
    first_token = plane_rank * tokens
    total_tokens = tokens * (slot_image_ref.shape[0] // (slots_here * PLANE))

    lane = lax.broadcasted_iota(jnp.int32, (own, head_dim), 1)
    starts = jnp.full((own, head_dim), total_tokens, jnp.int32)
    for image in range(n_images):
        starts = jnp.where(lane == image, image_start_ref[image], starts)
    for at, one in enumerate(order_of(member)):
        position = (
            first_token + one * own + lax.broadcasted_iota(jnp.int32, (own, head_dim), 0)
        )
        late_ref[at * own : (at + 1) * own] = jnp.where(starts > position, 1.0, 0.0).astype(
            jnp.bfloat16
        )

    step, several = SOURCES[0]
    for at, turn in enumerate(several):
        rank = source_rank(plane_rank, step, turn)
        for here in range(slots_here):
            image = slot_image_ref[(rank * PLANE + member) * slots_here + here]
            put_slot(keys_ref, values_ref, at * slots_here + here, kv_ref, at, here, image)
    sums_ref[...] = jnp.zeros_like(sums_ref)
    column = lax.broadcasted_iota(jnp.int32, sums_ref.shape, 1)
    keys = keys_ref[...].reshape(-1, 2 * head_dim)
    values = values_ref[...].reshape(-1, 2 * head_dim)
    together = 2

    def some_heads(number, _):
        several = [number * together + i for i in range(together)]
        totals = weigh(q_refs, halves, heads, several, late_ref[...], keys, values, scale)
        sums = sums_ref[...]
        for head, total in zip(several, totals):
            at = pl.ds(pl.multiple_of(head * head_dim, head_dim), head_dim)
            numer_ref[:, at] = total[:, :head_dim].astype(numer_ref.dtype)
            sums = jnp.where(column == head, total[:, head_dim:], sums)
        sums_ref[...] = sums
        return 0

    lax.fori_loop(0, heads // together, some_heads, 0, unroll=2)


def attend_last_kernel(
    image_start_ref, slot_image_ref, place_ref, *refs, scale, group, slots_here, heads, halves
):
    sources = SOURCES[1:]
    kv_refs, q_refs = refs[: len(sources)], refs[len(sources) : len(sources) + PLANE]
    numer_ref, came_ref, late_ref, kept_ref, to_core_ref = refs[len(sources) + PLANE : -3]
    keys_ref, values_ref, sums_ref = refs[-3:]
    _, own, head_dim = q_refs[0].shape
    n_images = image_start_ref.shape[0]
    plane_rank = place_ref[0]
    limit = (plane_rank + 1) * PLANE * own

    put = functools.partial(put_slot, keys_ref, values_ref)
    kept = jnp.int32(0)
    for kv_ref, (step, several) in zip(kv_refs, sources):
        for at, turn in enumerate(several):
            rank = source_rank(plane_rank, step, turn)
            for here in range(slots_here):
                image = slot_image_ref[(rank * PLANE + place_ref[1]) * slots_here + here]
                start = image_start_ref[jnp.minimum(image, n_images - 1)]
                seen = jnp.logical_and(image < n_images, start < limit)
                pl.when(seen)(functools.partial(put, kept, kv_ref, at, here, image))
                kept = kept + seen.astype(jnp.int32)
    turns = (kept + group - 1) // group

    def fill(to, _):
        put(to, kv_refs[0], 0, 0, n_images)
        return 0

    lax.fori_loop(kept, turns * group, fill, 0)
    sums_ref[...] = came_ref[...]
    column = lax.broadcasted_iota(jnp.int32, sums_ref.shape, 1)
    half = 2 * own

    def one_head(head, _, count):
        keys = keys_ref[:count].reshape(-1, 2 * head_dim)
        values = values_ref[:count].reshape(-1, 2 * head_dim)
        [total] = weigh(q_refs, halves, heads, [head], late_ref[...], keys, values, scale)
        at = pl.ds(pl.multiple_of(head * head_dim, head_dim), head_dim)
        numer = (numer_ref[:, at].astype(jnp.float32) + total[:, :head_dim]).astype(jnp.bfloat16)
        kept_ref[:, at] = numer[:half]
        to_core_ref[:, at] = numer[half:]
        sums = sums_ref[...]
        sums_ref[...] = jnp.where(column == head, sums + total[:, head_dim:], sums)
        return 0

    for turn in range(1, keys_ref.shape[0] // group + 1):

        @pl.when(turns == turn)
        def _():
            lax.fori_loop(
                0, heads, functools.partial(one_head, count=turn * group), 0, unroll=2
            )

    @pl.when(turns == 0)
    def _():
        kept_ref[:, : heads * head_dim] = numer_ref[:half]
        to_core_ref[:, : heads * head_dim] = numer_ref[half:]

    sums = split_sums(sums_ref[...], heads).astype(jnp.bfloat16)
    kept_ref[:, heads * head_dim :] = sums[:half]
    to_core_ref[:, heads * head_dim :] = sums[half:]


def add_kernel(kept_ref, came_ref, out_ref, *, heads):
    own, width = out_ref.shape
    cut = width - 128
    for first in range(0, cut, 256):
        columns = slice(first, min(first + 256, cut))
        out_ref[:, columns] = (
            kept_ref[own:, columns].astype(jnp.float32)
            + came_ref[own:, columns].astype(jnp.float32)
        ).astype(out_ref.dtype)
    sums = kept_ref[own:, cut:].astype(jnp.float32) + came_ref[own:, cut:].astype(jnp.float32)
    out_ref[:, cut:] = split_sums(join_sums(sums, heads), heads).astype(out_ref.dtype)


def combine_kernel(image_start_ref, place_ref, gate_ref, kept_ref, core_ref, chip_ref, out_ref):
    own, out_width = out_ref.shape
    width = kept_ref.shape[1]
    head_dim = width - out_width
    heads = out_width // head_dim
    first = (place_ref[0] * PLANE + place_ref[1]) * own
    position = first + lax.broadcasted_iota(jnp.int32, (own, 1), 0)
    seen = position >= image_start_ref[0]
    factor = jnp.tanh(gate_ref[...])

    def total(columns):
        return (
            kept_ref[:own, columns].astype(jnp.float32)
            + core_ref[:own, columns].astype(jnp.float32)
            + chip_ref[:, columns].astype(jnp.float32)
        )

    sums = join_sums(total(slice(out_width, width)), heads)
    share = jnp.where(seen, factor / jnp.where(seen, sums, 1.0), 0.0)
    for head in range(heads):
        columns = slice(head * head_dim, (head + 1) * head_dim)
        out_ref[:, columns] = (total(columns) * share[:, head : head + 1]).astype(out_ref.dtype)


def gather_along_z(block, beside=None):
    ctx_size = lax.axis_size("ctx")
    ranks = ctx_size // PLANE

    def shift(value, *distances):
        moves = [distances[i % len(distances)] * PLANE for i in range(ctx_size)]
        return lax.ppermute(
            value, "ctx", [(i, (i + moves[i]) % ctx_size) for i in range(ctx_size)]
        )

    groups = [
        [rank * PLANE + member for rank in range(first, ranks, STRIDE)]
        for member in range(PLANE)
        for first in range(STRIDE)
    ]
    own = lax.all_gather(block, "ctx", axis_index_groups=groups)
    if beside is not None:
        own, beside = lax.optimization_barrier((own, beside))
    return (own, shift(own, 1), shift(own, -1), shift(own, 2, -2)), beside


def other_member(value, mask):
    ctx_size = lax.axis_size("ctx")
    return lax.ppermute(value, "ctx", [(i, i ^ mask) for i in range(ctx_size)])


def local(
    queries,
    q_gain,
    k_gain,
    attn_gate,
    vision,
    key_projection_matrix,
    value_projection_matrix,
    image_start,
    slot_image,
):
    ctx_size = lax.axis_size("ctx")
    head_size = lax.axis_size("head")
    ranks = ctx_size // PLANE
    own_index = lax.axis_index("ctx")
    plane_rank = own_index // PLANE
    member = own_index % PLANE
    place = jnp.stack([plane_rank, member]).astype(jnp.int32)
    head_dim = q_gain.shape[0]
    tokens, q_cols = queries.shape
    heads = q_cols // head_dim
    rows, features = vision.shape
    piece_rows, kv_cols = key_projection_matrix.shape
    in_plane = [[rank * PLANE + m for m in range(PLANE)] for rank in range(ranks)]
    whole_plane = [
        [rank * PLANE * head_size + i for i in range(PLANE * head_size)] for rank in range(ranks)
    ]

    with jax.named_scope("norm_queries"):
        normed = pl.pallas_call(
            query_kernel,
            out_shape=jax.ShapeDtypeStruct((heads, tokens, head_dim), jnp.bfloat16),
            in_specs=[vmem(), vmem()],
            out_specs=vmem(),
            compiler_params=params(),
        )(queries, q_gain.reshape(1, head_dim))

    with jax.named_scope("spread_vision"):
        blocks = features // (piece_rows * PLANE)
        mine = pl.pallas_call(
            spread_kernel,
            out_shape=jax.ShapeDtypeStruct(
                (PLANE, head_size, blocks, rows, piece_rows), jnp.bfloat16
            ),
            in_specs=[vmem()],
            out_specs=pl.BlockSpec(memory_space=pltpu.HBM),
            scratch_shapes=[
                pltpu.VMEM((PLANE, blocks, rows, piece_rows), jnp.bfloat16),
                pltpu.SemaphoreType.DMA((PLANE * head_size,)),
            ],
            compiler_params=pltpu.CompilerParams(vmem_limit_bytes=SPREAD_LIMIT),
        )(vision)
        mine = mine.reshape(PLANE * head_size, blocks, rows, piece_rows)
        spread = lax.all_to_all(mine, ("ctx", "head"), 0, 0, axis_index_groups=whole_plane)
        spread = spread.reshape(PLANE, ranks, rows, piece_rows)

    with jax.named_scope("gather_projections"):
        weights, _ = gather_along_z(
            jnp.concatenate([key_projection_matrix, value_projection_matrix], axis=1)
        )

    with jax.named_scope("share_queries"):
        core_queries = other_member(normed, 1)
        spread, core_queries = lax.optimization_barrier((spread, core_queries))
        chip_queries = other_member(jnp.concatenate([normed, core_queries]), 2)

    with jax.named_scope("project"):
        partial = pl.pallas_call(
            project_first_kernel,
            out_shape=jax.ShapeDtypeStruct((PLANE * rows, 2 * kv_cols), jnp.float32),
            in_specs=[smem()] + [vmem()] * (1 + FIRST),
            out_specs=vmem(),
            compiler_params=params(),
        )(place, spread, *weights[:FIRST])
        triple = 3 * kv_cols
        shapes = [(rows, triple), (rows, triple), (2 * rows, triple)]
        kept, to_chip, to_core = pl.pallas_call(
            project_last_kernel,
            out_shape=[jax.ShapeDtypeStruct(shape, jnp.bfloat16) for shape in shapes],
            in_specs=[smem()] + [vmem()] * (2 + len(weights) - FIRST),
            out_specs=[vmem()] * 3,
            compiler_params=params(),
        )(place, spread, *weights[FIRST:], partial)

    with jax.named_scope("sum_projections"):
        from_core = other_member(to_core, 1)
        to_chip = pl.pallas_call(
            add_products_kernel,
            out_shape=jax.ShapeDtypeStruct((rows, triple), jnp.bfloat16),
            in_specs=[vmem()] * 2,
            out_specs=vmem(),
            compiler_params=params(),
        )(to_chip, from_core)
        from_chip = other_member(to_chip, 2)
        own_kv = pl.pallas_call(
            finish_kernel,
            out_shape=jax.ShapeDtypeStruct((rows, 2 * kv_cols), jnp.bfloat16),
            in_specs=[vmem()] * 4,
            out_specs=vmem(),
            compiler_params=params(),
        )(kept, from_core, from_chip, k_gain.reshape(1, head_dim))

    with jax.named_scope("gather_keys_values"):
        all_kv, chip_queries = gather_along_z(own_kv, chip_queries)

    with jax.named_scope("attend"):
        slots_here = slot_image.shape[0] // ctx_size
        tile_rows = rows // slots_here
        slots = slots_here * len(SOURCES[0][1])
        last_slots = ranks * slots_here - slots
        group = math.gcd(last_slots, 4)
        width = q_cols + head_dim
        scale = head_dim ** (-0.5) * math.log2(math.e)
        plane_queries = [(normed, 0), (chip_queries, 0), (core_queries, 0), (chip_queries, 1)]

        def cost(rows_here, slots):
            scores = heads * rows_here * slots * tile_rows
            return pl.CostEstimate(
                flops=8 * scores * head_dim,
                bytes_accessed=4 * rows_here * width,
                transcendentals=scores,
            )

        numer, sums, late = pl.pallas_call(
            functools.partial(
                attend_first_kernel,
                scale=scale,
                slots_here=slots_here,
                heads=heads,
                halves=tuple(half for _, half in plane_queries),
            ),
            out_shape=[
                jax.ShapeDtypeStruct((PLANE * tokens, q_cols), jnp.bfloat16),
                jax.ShapeDtypeStruct((PLANE * tokens, head_dim), jnp.float32),
                jax.ShapeDtypeStruct((PLANE * tokens, head_dim), jnp.bfloat16),
            ],
            in_specs=[smem()] * 3 + [vmem()] * (1 + PLANE),
            out_specs=[vmem()] * 3,
            scratch_shapes=[pltpu.VMEM((slots, tile_rows, 2 * head_dim), jnp.bfloat16)] * 2,
            compiler_params=params(),
            cost_estimate=cost(PLANE * tokens, slots),
        )(
            image_start,
            slot_image,
            place,
            all_kv[0],
            *(source for source, _ in plane_queries),
        )
        own_and_chip, to_core = pl.pallas_call(
            functools.partial(
                attend_last_kernel,
                scale=scale,
                group=group,
                slots_here=slots_here,
                heads=heads,
                halves=tuple(half for _, half in plane_queries),
            ),
            out_shape=[jax.ShapeDtypeStruct((2 * tokens, width), jnp.bfloat16)] * 2,
            in_specs=[smem()] * 3 + [vmem()] * (len(all_kv) - 1 + PLANE + 3),
            out_specs=[vmem()] * 2,
            scratch_shapes=[
                pltpu.VMEM((last_slots, tile_rows, 2 * head_dim), jnp.bfloat16),
                pltpu.VMEM((last_slots, tile_rows, 2 * head_dim), jnp.bfloat16),
                pltpu.VMEM((PLANE * tokens, head_dim), jnp.float32),
            ],
            compiler_params=params(),
            cost_estimate=cost(PLANE * tokens, last_slots),
        )(
            image_start,
            slot_image,
            place,
            *all_kv[1:],
            *(source for source, _ in plane_queries),
            numer,
            sums,
            late,
        )
        from_core = other_member(to_core, 1)

    with jax.named_scope("sum_attention"):
        to_chip = pl.pallas_call(
            functools.partial(add_kernel, heads=heads),
            out_shape=jax.ShapeDtypeStruct((tokens, width), jnp.bfloat16),
            in_specs=[vmem(), vmem()],
            out_specs=vmem(),
            compiler_params=params(),
        )(own_and_chip, from_core)
        from_chip = other_member(to_chip, 2)
        return pl.pallas_call(
            combine_kernel,
            out_shape=jax.ShapeDtypeStruct((tokens, q_cols), jnp.bfloat16),
            in_specs=[smem(), smem()] + [vmem()] * 4,
            out_specs=vmem(),
            compiler_params=params(),
        )(image_start, place, attn_gate.reshape(1, 1), own_and_chip, from_core, from_chip)


def solution(mesh):
    in_specs = (
        P("ctx", "head"),
        P(),
        P(),
        P(),
        P("ctx", "head"),
        P("ctx", "head"),
        P("ctx", "head"),
        P(),
        P(),
    )
    out_specs = P("ctx", "head")
    return jax.shard_map(local, mesh=mesh, in_specs=in_specs, out_specs=out_specs, check_vma=False)
```

```python
import functools
import math

import jax
import jax.numpy as jnp
from jax import lax
from jax.experimental import pallas as pl
from jax.experimental.pallas import tpu as pltpu
from jax.sharding import PartitionSpec as P

EPS = 1e-05
PLANE = 4
VMEM_LIMIT = 16 * 1024 * 1024
SPREAD_LIMIT = 62 * 1024 * 1024
NO_IMAGE = 127
HIDE = -30000.0
STRIDE = 4
SOURCES = ((0, (0, 1, 2, 3)), (2, (0, 1, 2, 3)), (-1, (0, 1, 2, 3)), (1, (0, 1, 2, 3)))

FIRST = 2


def source_rank(plane_rank, step, turn):
    return lax.rem(plane_rank + step + STRIDE, STRIDE) + STRIDE * turn


def params(**more):
    return pltpu.CompilerParams(vmem_limit_bytes=VMEM_LIMIT, **more)


def vmem():
    return pl.BlockSpec(memory_space=pltpu.VMEM)


def smem():
    return pl.BlockSpec(memory_space=pltpu.SMEM)


def spread_kernel(x_ref, out_ref, pieces_ref, sems):
    members, peers, blocks, _, width = out_ref.shape
    copies = []
    for member in range(members):
        for block in range(blocks):
            first = (block * members + member) * width
            piece = x_ref[:, first : first + width]
            for peer in range(peers):
                pieces_ref[member, peer, block] = piece
        copies.append(
            pltpu.make_async_copy(pieces_ref.at[member], out_ref.at[member], sems.at[member])
        )
        copies[-1].start()
    for copy in copies:
        copy.wait()


def order_of(member):
    return member, member ^ 2, member ^ 1, member ^ 3


def products(place_ref, x_ref, weight_refs, sources):
    depth = x_ref.shape[3]
    total = None
    for ref, (step, several) in zip(weight_refs, sources):
        for at in range(0, len(several), 2):
            both = [source_rank(place_ref[0], step, several[at + i]) for i in range(2)]
            part = jnp.dot(
                jnp.concatenate(
                    [
                        jnp.concatenate([x_ref[member, rank] for rank in both], axis=1)
                        for member in order_of(place_ref[1])
                    ],
                    axis=0,
                ),
                ref[at : at + 2].reshape(2 * depth, ref.shape[2]),
                preferred_element_type=jnp.float32,
            )
            total = part if total is None else total + part
    return total


def project_first_kernel(place_ref, x_ref, *refs):
    refs[-1][...] = products(place_ref, x_ref, refs[:-1], SOURCES[:FIRST])


def pack_products(total):
    head_dim = total.shape[1] // 2
    keys = total[:, :head_dim]
    high = keys.astype(jnp.bfloat16)
    low = (keys - high.astype(jnp.float32)).astype(jnp.bfloat16)
    return jnp.concatenate([high, low, total[:, head_dim:].astype(jnp.bfloat16)], axis=1)


def unpack_products(parts):
    head_dim = parts.shape[1] // 3
    parts = parts.astype(jnp.float32)
    keys = parts[:, :head_dim] + parts[:, head_dim : 2 * head_dim]
    return jnp.concatenate([keys, parts[:, 2 * head_dim :]], axis=1)


def project_last_kernel(place_ref, x_ref, *refs):
    weight_refs, first_ref, out_refs = refs[:-4], refs[-4], refs[-3:]
    total = first_ref[...] + products(place_ref, x_ref, weight_refs, SOURCES[FIRST:])
    packed = pack_products(total)
    rows = x_ref.shape[2]
    for out_ref, (start, stop) in zip(out_refs, ((0, 1), (1, 2), (2, 4))):
        out_ref[...] = packed[start * rows : stop * rows]


def add_products_kernel(kept_ref, came_ref, out_ref):
    rows = kept_ref.shape[0]
    out_ref[...] = pack_products(
        unpack_products(kept_ref[...]) + unpack_products(came_ref[rows:])
    )


def finish_kernel(kept_ref, core_ref, chip_ref, gain_ref, out_ref):
    rows = kept_ref.shape[0]
    raw = (
        unpack_products(kept_ref[...])
        + unpack_products(core_ref[:rows])
        + unpack_products(chip_ref[...])
    )
    head_dim = gain_ref.shape[1]
    keys = raw[:, :head_dim]
    mean = jnp.mean(keys * keys, axis=-1, keepdims=True)
    keys = keys * lax.rsqrt(mean + EPS) * gain_ref[...]
    out_ref[...] = jnp.concatenate([keys, raw[:, head_dim:]], axis=1).astype(out_ref.dtype)


def query_kernel(q_ref, gain_ref, out_ref):
    heads, _, head_dim = out_ref.shape
    for head in range(heads):
        raw = q_ref[:, head * head_dim : (head + 1) * head_dim].astype(jnp.float32)
        mean = jnp.mean(raw * raw, axis=-1, keepdims=True)
        out_ref[head] = (raw * lax.rsqrt(mean + EPS) * gain_ref[...]).astype(out_ref.dtype)


def split_sums(sums, heads):
    column = lax.broadcasted_iota(jnp.int32, sums.shape, 1)
    high = sums.astype(jnp.bfloat16).astype(jnp.float32)
    low = pltpu.roll(sums - high, heads, 1)
    return jnp.where(column < heads, high, jnp.where(column < 2 * heads, low, 0.0))


def join_sums(parts, heads):
    return parts + pltpu.roll(parts, parts.shape[1] - heads, 1)


def put_slot(keys_ref, values_ref, to, kv_ref, at, here, image):
    _, tile_rows, width = keys_ref.shape
    head_dim = width // 2
    rows = slice(here * tile_rows, (here + 1) * tile_rows)
    lane = lax.broadcasted_iota(jnp.int32, (tile_rows, head_dim), 1)
    mark = jnp.where(lane == image, HIDE, 0.0).astype(jnp.bfloat16)
    ones = jnp.ones((tile_rows, head_dim), jnp.bfloat16)
    keys_ref[to] = jnp.concatenate([kv_ref[at, rows, :head_dim], mark], axis=1)
    values_ref[to] = jnp.concatenate([kv_ref[at, rows, head_dim:], ones], axis=1)


def weigh(queries, keys, values, scale):
    scores = lax.dot_general(
        queries, keys, (((1,), (1,)), ((), ())), preferred_element_type=jnp.float32
    )
    weights = jnp.exp2(scores * scale).astype(jnp.bfloat16)
    return jnp.dot(weights, values, preferred_element_type=jnp.float32)


def attend_first_kernel(
    image_start_ref, slot_image_ref, place_ref, *refs, scale, slots_here, halves
):
    kv_ref, q_refs = refs[0], refs[1 : 1 + PLANE]
    numer_ref, sums_ref, marked_ref, plan_ref, keys_ref, values_ref = refs[1 + PLANE :]
    _, own, head_dim = q_refs[0].shape
    heads = marked_ref.shape[0]
    n_images = image_start_ref.shape[0]
    tokens = PLANE * own
    plane_rank = place_ref[0]
    member = place_ref[1]
    first_token = plane_rank * tokens
    total_tokens = tokens * (slot_image_ref.shape[0] // (slots_here * PLANE))

    kept = jnp.int32(0)
    number = 0
    for step, several in SOURCES[1:]:
        for turn in several:
            rank = source_rank(plane_rank, step, turn)
            for here in range(slots_here):
                image = slot_image_ref[(rank * PLANE + member) * slots_here + here]
                start = image_start_ref[jnp.minimum(image, n_images - 1)]
                seen = jnp.logical_and(image < n_images, start < first_token + tokens)
                plan_ref[2 * number] = image
                plan_ref[2 * number + 1] = jnp.where(seen, kept, -1)
                kept = kept + seen.astype(jnp.int32)
                number += 1
    plan_ref[2 * number] = kept

    lane = lax.broadcasted_iota(jnp.int32, (own, head_dim), 1)
    starts = jnp.full((own, head_dim), total_tokens, jnp.int32)
    for image in range(n_images):
        starts = jnp.where(lane == image, image_start_ref[image], starts)
    for at, one in enumerate(order_of(member)):
        position = (
            first_token + one * own + lax.broadcasted_iota(jnp.int32, (own, head_dim), 0)
        )
        late = jnp.where(starts > position, 1.0, 0.0).astype(jnp.bfloat16)
        rows = slice(at * own, (at + 1) * own)
        for head in range(heads):
            marked_ref[head, rows, :head_dim] = q_refs[at][halves[at] * heads + head]
            marked_ref[head, rows, head_dim:] = late

    step, several = SOURCES[0]
    for at, turn in enumerate(several):
        rank = source_rank(plane_rank, step, turn)
        for here in range(slots_here):
            image = slot_image_ref[(rank * PLANE + member) * slots_here + here]
            put_slot(keys_ref, values_ref, at * slots_here + here, kv_ref, at, here, image)
    sums_ref[...] = jnp.zeros_like(sums_ref)
    column = lax.broadcasted_iota(jnp.int32, sums_ref.shape, 1)
    keys = keys_ref[...].reshape(-1, 2 * head_dim)
    values = values_ref[...].reshape(-1, 2 * head_dim)

    def one_head(head, _):
        total = weigh(marked_ref[head], keys, values, scale)
        at = pl.ds(pl.multiple_of(head * head_dim, head_dim), head_dim)
        numer_ref[:, at] = total[:, :head_dim].astype(numer_ref.dtype)
        sums_ref[...] = jnp.where(column == head, total[:, head_dim:], sums_ref[...])
        return 0

    lax.fori_loop(0, heads, one_head, 0, unroll=2)


def attend_last_kernel(plan_ref, *refs, scale, group, slots_here):
    sources = SOURCES[1:]
    kv_refs = refs[: len(sources)]
    numer_ref, came_ref, marked_ref, kept_ref, to_core_ref = refs[len(sources) : -3]
    keys_ref, values_ref, sums_ref = refs[-3:]
    heads, tokens, width = marked_ref.shape
    head_dim = width // 2

    put = functools.partial(put_slot, keys_ref, values_ref)
    number = 0
    for kv_ref, (_, several) in zip(kv_refs, sources):
        for at in range(len(several)):
            for here in range(slots_here):
                image, to = plan_ref[2 * number], plan_ref[2 * number + 1]
                pl.when(to >= 0)(functools.partial(put, to, kv_ref, at, here, image))
                number += 1
    kept = plan_ref[2 * number]
    turns = (kept + group - 1) // group

    def fill(to, _):
        put(to, kv_refs[0], 0, 0, NO_IMAGE)
        return 0

    lax.fori_loop(kept, turns * group, fill, 0)
    sums_ref[...] = came_ref[...]
    column = lax.broadcasted_iota(jnp.int32, sums_ref.shape, 1)
    half = tokens // 2

    def one_head(head, _, count):
        keys = keys_ref[:count].reshape(-1, 2 * head_dim)
        values = values_ref[:count].reshape(-1, 2 * head_dim)
        total = weigh(marked_ref[head], keys, values, scale)
        at = pl.ds(pl.multiple_of(head * head_dim, head_dim), head_dim)
        numer = (numer_ref[:, at].astype(jnp.float32) + total[:, :head_dim]).astype(jnp.bfloat16)
        kept_ref[:, at] = numer[:half]
        to_core_ref[:, at] = numer[half:]
        sums = sums_ref[...]
        sums_ref[...] = jnp.where(column == head, sums + total[:, head_dim:], sums)
        return 0

    for turn in range(1, keys_ref.shape[0] // group + 1):

        @pl.when(turns == turn)
        def _():
            lax.fori_loop(
                0, heads, functools.partial(one_head, count=turn * group), 0, unroll=2
            )

    @pl.when(turns == 0)
    def _():
        kept_ref[:, : heads * head_dim] = numer_ref[:half]
        to_core_ref[:, : heads * head_dim] = numer_ref[half:]

    sums = split_sums(sums_ref[...], heads).astype(jnp.bfloat16)
    kept_ref[:, heads * head_dim :] = sums[:half]
    to_core_ref[:, heads * head_dim :] = sums[half:]


def add_kernel(kept_ref, came_ref, out_ref, *, heads):
    own, width = out_ref.shape
    cut = width - 128
    for first in range(0, cut, 256):
        columns = slice(first, min(first + 256, cut))
        out_ref[:, columns] = (
            kept_ref[own:, columns].astype(jnp.float32)
            + came_ref[own:, columns].astype(jnp.float32)
        ).astype(out_ref.dtype)
    sums = kept_ref[own:, cut:].astype(jnp.float32) + came_ref[own:, cut:].astype(jnp.float32)
    out_ref[:, cut:] = split_sums(join_sums(sums, heads), heads).astype(out_ref.dtype)


def combine_kernel(image_start_ref, place_ref, gate_ref, kept_ref, core_ref, chip_ref, out_ref):
    own, out_width = out_ref.shape
    width = kept_ref.shape[1]
    head_dim = width - out_width
    heads = out_width // head_dim
    first = (place_ref[0] * PLANE + place_ref[1]) * own
    position = first + lax.broadcasted_iota(jnp.int32, (own, 1), 0)
    seen = position >= image_start_ref[0]
    factor = jnp.tanh(gate_ref[...])

    def total(columns):
        return (
            kept_ref[:own, columns].astype(jnp.float32)
            + core_ref[:own, columns].astype(jnp.float32)
            + chip_ref[:, columns].astype(jnp.float32)
        )

    sums = join_sums(total(slice(out_width, width)), heads)
    share = jnp.where(seen, factor / jnp.where(seen, sums, 1.0), 0.0)
    for head in range(heads):
        columns = slice(head * head_dim, (head + 1) * head_dim)
        out_ref[:, columns] = (total(columns) * share[:, head : head + 1]).astype(out_ref.dtype)


def gather_along_z(block, beside=None):
    ctx_size = lax.axis_size("ctx")
    ranks = ctx_size // PLANE

    def shift(value, *distances):
        moves = [distances[i % len(distances)] * PLANE for i in range(ctx_size)]
        return lax.ppermute(
            value, "ctx", [(i, (i + moves[i]) % ctx_size) for i in range(ctx_size)]
        )

    groups = [
        [rank * PLANE + member for rank in range(first, ranks, STRIDE)]
        for member in range(PLANE)
        for first in range(STRIDE)
    ]
    own = lax.all_gather(block, "ctx", axis_index_groups=groups)
    if beside is not None:
        own, beside = lax.optimization_barrier((own, beside))
    return (own, shift(own, 2, -2), shift(own, 1), shift(own, -1)), beside


def other_member(value, mask):
    ctx_size = lax.axis_size("ctx")
    return lax.ppermute(value, "ctx", [(i, i ^ mask) for i in range(ctx_size)])


def local(
    queries,
    q_gain,
    k_gain,
    attn_gate,
    vision,
    key_projection_matrix,
    value_projection_matrix,
    image_start,
    slot_image,
):
    ctx_size = lax.axis_size("ctx")
    head_size = lax.axis_size("head")
    ranks = ctx_size // PLANE
    own_index = lax.axis_index("ctx")
    plane_rank = own_index // PLANE
    member = own_index % PLANE
    place = jnp.stack([plane_rank, member]).astype(jnp.int32)
    head_dim = q_gain.shape[0]
    tokens, q_cols = queries.shape
    heads = q_cols // head_dim
    rows, features = vision.shape
    piece_rows, kv_cols = key_projection_matrix.shape
    in_plane = [[rank * PLANE + m for m in range(PLANE)] for rank in range(ranks)]
    whole_plane = [
        [rank * PLANE * head_size + i for i in range(PLANE * head_size)] for rank in range(ranks)
    ]

    with jax.named_scope("norm_queries"):
        normed = pl.pallas_call(
            query_kernel,
            out_shape=jax.ShapeDtypeStruct((heads, tokens, head_dim), jnp.bfloat16),
            in_specs=[vmem(), vmem()],
            out_specs=vmem(),
            compiler_params=params(),
        )(queries, q_gain.reshape(1, head_dim))

    with jax.named_scope("spread_vision"):
        blocks = features // (piece_rows * PLANE)
        mine = pl.pallas_call(
            spread_kernel,
            out_shape=jax.ShapeDtypeStruct(
                (PLANE, head_size, blocks, rows, piece_rows), jnp.bfloat16
            ),
            in_specs=[vmem()],
            out_specs=pl.BlockSpec(memory_space=pltpu.HBM),
            scratch_shapes=[
                pltpu.VMEM((PLANE, head_size, blocks, rows, piece_rows), jnp.bfloat16),
                pltpu.SemaphoreType.DMA((PLANE,)),
            ],
            compiler_params=pltpu.CompilerParams(vmem_limit_bytes=SPREAD_LIMIT),
        )(vision)
        mine = mine.reshape(PLANE * head_size, blocks, rows, piece_rows)
        spread = lax.all_to_all(mine, ("ctx", "head"), 0, 0, axis_index_groups=whole_plane)
        spread = spread.reshape(PLANE, ranks, rows, piece_rows)

    with jax.named_scope("gather_projections"):
        weights, _ = gather_along_z(
            jnp.concatenate([key_projection_matrix, value_projection_matrix], axis=1)
        )

    with jax.named_scope("share_queries"):
        core_queries = other_member(normed, 1)
        spread, core_queries = lax.optimization_barrier((spread, core_queries))
        chip_queries = other_member(jnp.concatenate([normed, core_queries]), 2)

    with jax.named_scope("project"):
        partial = pl.pallas_call(
            project_first_kernel,
            out_shape=jax.ShapeDtypeStruct((PLANE * rows, 2 * kv_cols), jnp.float32),
            in_specs=[smem()] + [vmem()] * (1 + FIRST),
            out_specs=vmem(),
            compiler_params=params(),
        )(place, spread, *weights[:FIRST])
        triple = 3 * kv_cols
        shapes = [(rows, triple), (rows, triple), (2 * rows, triple)]
        kept, to_chip, to_core = pl.pallas_call(
            project_last_kernel,
            out_shape=[jax.ShapeDtypeStruct(shape, jnp.bfloat16) for shape in shapes],
            in_specs=[smem()] + [vmem()] * (2 + len(weights) - FIRST),
            out_specs=[vmem()] * 3,
            compiler_params=params(),
        )(place, spread, *weights[FIRST:], partial)

    with jax.named_scope("sum_projections"):
        from_core = other_member(to_core, 1)
        to_chip = pl.pallas_call(
            add_products_kernel,
            out_shape=jax.ShapeDtypeStruct((rows, triple), jnp.bfloat16),
            in_specs=[vmem()] * 2,
            out_specs=vmem(),
            compiler_params=params(),
        )(to_chip, from_core)
        from_chip = other_member(to_chip, 2)
        own_kv = pl.pallas_call(
            finish_kernel,
            out_shape=jax.ShapeDtypeStruct((rows, 2 * kv_cols), jnp.bfloat16),
            in_specs=[vmem()] * 4,
            out_specs=vmem(),
            compiler_params=params(),
        )(kept, from_core, from_chip, k_gain.reshape(1, head_dim))

    with jax.named_scope("gather_keys_values"):
        all_kv, chip_queries = gather_along_z(own_kv, chip_queries)

    with jax.named_scope("attend"):
        slots_here = slot_image.shape[0] // ctx_size
        tile_rows = rows // slots_here
        slots = slots_here * len(SOURCES[0][1])
        last_slots = ranks * slots_here - slots
        group = math.gcd(last_slots, 4)
        width = q_cols + head_dim
        scale = head_dim ** (-0.5) * math.log2(math.e)
        plane_queries = [(normed, 0), (chip_queries, 0), (core_queries, 0), (chip_queries, 1)]

        def cost(rows_here, slots):
            scores = heads * rows_here * slots * tile_rows
            return pl.CostEstimate(
                flops=8 * scores * head_dim,
                bytes_accessed=4 * rows_here * width,
                transcendentals=scores,
            )

        numer, sums, marked, plan = pl.pallas_call(
            functools.partial(
                attend_first_kernel,
                scale=scale,
                slots_here=slots_here,
                halves=tuple(half for _, half in plane_queries),
            ),
            out_shape=[
                jax.ShapeDtypeStruct((PLANE * tokens, q_cols), jnp.bfloat16),
                jax.ShapeDtypeStruct((PLANE * tokens, head_dim), jnp.float32),
                jax.ShapeDtypeStruct((heads, PLANE * tokens, 2 * head_dim), jnp.bfloat16),
                jax.ShapeDtypeStruct((2 * last_slots + 1,), jnp.int32),
            ],
            in_specs=[smem()] * 3 + [vmem()] * (1 + PLANE),
            out_specs=[vmem()] * 3 + [smem()],
            scratch_shapes=[pltpu.VMEM((slots, tile_rows, 2 * head_dim), jnp.bfloat16)] * 2,
            compiler_params=params(),
            cost_estimate=cost(PLANE * tokens, slots),
        )(
            image_start,
            slot_image,
            place,
            all_kv[0],
            *(source for source, _ in plane_queries),
        )
        own_and_chip, to_core = pl.pallas_call(
            functools.partial(
                attend_last_kernel, scale=scale, group=group, slots_here=slots_here
            ),
            out_shape=[jax.ShapeDtypeStruct((2 * tokens, width), jnp.bfloat16)] * 2,
            in_specs=[smem()] + [vmem()] * (len(all_kv) - 1 + 3),
            out_specs=[vmem()] * 2,
            scratch_shapes=[
                pltpu.VMEM((last_slots, tile_rows, 2 * head_dim), jnp.bfloat16),
                pltpu.VMEM((last_slots, tile_rows, 2 * head_dim), jnp.bfloat16),
                pltpu.VMEM((PLANE * tokens, head_dim), jnp.float32),
            ],
            compiler_params=params(),
            cost_estimate=cost(PLANE * tokens, last_slots),
        )(plan, *all_kv[1:], numer, sums, marked)
        from_core = other_member(to_core, 1)

    with jax.named_scope("sum_attention"):
        to_chip = pl.pallas_call(
            functools.partial(add_kernel, heads=heads),
            out_shape=jax.ShapeDtypeStruct((tokens, width), jnp.bfloat16),
            in_specs=[vmem(), vmem()],
            out_specs=vmem(),
            compiler_params=params(),
        )(own_and_chip, from_core)
        from_chip = other_member(to_chip, 2)
        return pl.pallas_call(
            combine_kernel,
            out_shape=jax.ShapeDtypeStruct((tokens, q_cols), jnp.bfloat16),
            in_specs=[smem(), smem()] + [vmem()] * 4,
            out_specs=vmem(),
            compiler_params=params(),
        )(image_start, place, attn_gate.reshape(1, 1), own_and_chip, from_core, from_chip)


def solution(mesh):
    in_specs = (
        P("ctx", "head"),
        P(),
        P(),
        P(),
        P("ctx", "head"),
        P("ctx", "head"),
        P("ctx", "head"),
        P(),
        P(),
    )
    out_specs = P("ctx", "head")
    return jax.shard_map(local, mesh=mesh, in_specs=in_specs, out_specs=out_specs, check_vma=False)
```

```python
import functools
import math

import jax
import jax.numpy as jnp
from jax import lax
from jax.experimental import pallas as pl
from jax.experimental.pallas import tpu as pltpu
from jax.sharding import PartitionSpec as P

EPS = 1e-05
PLANE = 4
VMEM_LIMIT = 16 * 1024 * 1024
TOKEN_ORDER = (0, 2, 1, 3)
SPREAD_LIMIT = 62 * 1024 * 1024
NO_IMAGE = 127
HIDE = -30000.0
STRIDE = 4
SOURCES = ((0, (0, 1, 2, 3)), (2, (0, 1, 2, 3)), (-1, (0, 1, 2, 3)), (1, (0, 1, 2, 3)))

FIRST = 2


def source_rank(plane_rank, step, turn):
    return lax.rem(plane_rank + step + STRIDE, STRIDE) + STRIDE * turn


def params(**more):
    return pltpu.CompilerParams(vmem_limit_bytes=VMEM_LIMIT, **more)


def vmem():
    return pl.BlockSpec(memory_space=pltpu.VMEM)


def smem():
    return pl.BlockSpec(memory_space=pltpu.SMEM)


def spread_kernel(x_ref, out_ref, pieces_ref, sems):
    members, peers, blocks, _, width = out_ref.shape
    copies = []
    for member in range(members):
        for block in range(blocks):
            first = (block * members + member) * width
            piece = x_ref[:, first : first + width]
            for peer in range(peers):
                pieces_ref[member, peer, block] = piece
        copies.append(
            pltpu.make_async_copy(pieces_ref.at[member], out_ref.at[member], sems.at[member])
        )
        copies[-1].start()
    for copy in copies:
        copy.wait()


def order_of(member):
    return member, member ^ 2, member ^ 1, member ^ 3


def products(place_ref, x_ref, weight_refs, sources):
    depth = x_ref.shape[3]
    total = None
    for ref, (step, several) in zip(weight_refs, sources):
        for at in range(0, len(several), 2):
            both = [source_rank(place_ref[0], step, several[at + i]) for i in range(2)]
            part = jnp.dot(
                jnp.concatenate(
                    [
                        jnp.concatenate([x_ref[member, rank] for rank in both], axis=1)
                        for member in order_of(place_ref[1])
                    ],
                    axis=0,
                ),
                ref[at : at + 2].reshape(2 * depth, ref.shape[2]),
                preferred_element_type=jnp.float32,
            )
            total = part if total is None else total + part
    return total


def project_first_kernel(place_ref, x_ref, *refs):
    refs[-1][...] = products(place_ref, x_ref, refs[:-1], SOURCES[:FIRST])


def pack_products(total):
    head_dim = total.shape[1] // 2
    keys = total[:, :head_dim]
    high = keys.astype(jnp.bfloat16)
    low = (keys - high.astype(jnp.float32)).astype(jnp.bfloat16)
    return jnp.concatenate([high, low, total[:, head_dim:].astype(jnp.bfloat16)], axis=1)


def unpack_products(parts):
    head_dim = parts.shape[1] // 3
    parts = parts.astype(jnp.float32)
    keys = parts[:, :head_dim] + parts[:, head_dim : 2 * head_dim]
    return jnp.concatenate([keys, parts[:, 2 * head_dim :]], axis=1)


def project_last_kernel(place_ref, x_ref, *refs):
    weight_refs, first_ref, out_refs = refs[:-4], refs[-4], refs[-3:]
    total = first_ref[...] + products(place_ref, x_ref, weight_refs, SOURCES[FIRST:])
    packed = pack_products(total)
    rows = x_ref.shape[2]
    for out_ref, (start, stop) in zip(out_refs, ((0, 1), (1, 2), (2, 4))):
        out_ref[...] = packed[start * rows : stop * rows]


def add_products_kernel(kept_ref, came_ref, out_ref):
    rows = kept_ref.shape[0]
    out_ref[...] = pack_products(
        unpack_products(kept_ref[...]) + unpack_products(came_ref[rows:])
    )


def finish_kernel(kept_ref, core_ref, chip_ref, gain_ref, out_ref):
    rows = kept_ref.shape[0]
    raw = (
        unpack_products(kept_ref[...])
        + unpack_products(core_ref[:rows])
        + unpack_products(chip_ref[...])
    )
    head_dim = gain_ref.shape[1]
    keys = raw[:, :head_dim]
    mean = jnp.mean(keys * keys, axis=-1, keepdims=True)
    keys = keys * lax.rsqrt(mean + EPS) * gain_ref[...]
    out_ref[...] = jnp.concatenate([keys, raw[:, head_dim:]], axis=1).astype(out_ref.dtype)


def query_kernel(q_ref, gain_ref, out_ref):
    heads, _, head_dim = out_ref.shape
    for head in range(heads):
        raw = q_ref[:, head * head_dim : (head + 1) * head_dim].astype(jnp.float32)
        mean = jnp.mean(raw * raw, axis=-1, keepdims=True)
        out_ref[head] = (raw * lax.rsqrt(mean + EPS) * gain_ref[...]).astype(out_ref.dtype)


def split_sums(sums, heads):
    column = lax.broadcasted_iota(jnp.int32, sums.shape, 1)
    high = sums.astype(jnp.bfloat16).astype(jnp.float32)
    low = pltpu.roll(sums - high, heads, 1)
    return jnp.where(column < heads, high, jnp.where(column < 2 * heads, low, 0.0))


def join_sums(parts, heads):
    return parts + pltpu.roll(parts, parts.shape[1] - heads, 1)


def put_slot(keys_ref, values_ref, to, kv_ref, at, here, image):
    _, tile_rows, width = keys_ref.shape
    head_dim = width // 2
    rows = slice(here * tile_rows, (here + 1) * tile_rows)
    lane = lax.broadcasted_iota(jnp.int32, (tile_rows, head_dim), 1)
    mark = jnp.where(lane == image, HIDE, 0.0).astype(jnp.bfloat16)
    ones = jnp.ones((tile_rows, head_dim), jnp.bfloat16)
    keys_ref[to] = jnp.concatenate([kv_ref[at, rows, :head_dim], mark], axis=1)
    values_ref[to] = jnp.concatenate([kv_ref[at, rows, head_dim:], ones], axis=1)


def weigh(queries, keys, values, scale):
    scores = lax.dot_general(
        queries, keys, (((1,), (1,)), ((), ())), preferred_element_type=jnp.float32
    )
    weights = jnp.exp2(scores * scale).astype(jnp.bfloat16)
    return jnp.dot(weights, values, preferred_element_type=jnp.float32)


def attend_first_kernel(
    image_start_ref, slot_image_ref, place_ref, *refs, scale, slots_here, halves
):
    kv_ref, q_refs = refs[0], refs[1 : 1 + PLANE]
    numer_ref, sums_ref, marked_ref, plan_ref, keys_ref, values_ref = refs[1 + PLANE :]
    _, own, head_dim = q_refs[0].shape
    heads = marked_ref.shape[0]
    n_images = image_start_ref.shape[0]
    tokens = PLANE * own
    plane_rank = place_ref[0]
    member = place_ref[1]
    first_token = plane_rank * tokens
    total_tokens = tokens * (slot_image_ref.shape[0] // (slots_here * PLANE))

    kept = jnp.int32(0)
    number = 0
    for step, several in SOURCES[1:]:
        for turn in several:
            rank = source_rank(plane_rank, step, turn)
            for here in range(slots_here):
                image = slot_image_ref[(rank * PLANE + member) * slots_here + here]
                start = image_start_ref[jnp.minimum(image, n_images - 1)]
                seen = jnp.logical_and(image < n_images, start < first_token + tokens)
                plan_ref[2 * number] = image
                plan_ref[2 * number + 1] = jnp.where(seen, kept, -1)
                kept = kept + seen.astype(jnp.int32)
                number += 1
    plan_ref[2 * number] = kept

    lane = lax.broadcasted_iota(jnp.int32, (own, head_dim), 1)
    starts = jnp.full((own, head_dim), total_tokens, jnp.int32)
    for image in range(n_images):
        starts = jnp.where(lane == image, image_start_ref[image], starts)
    for at, mask in enumerate(TOKEN_ORDER):
        one = member ^ mask
        position = (
            first_token + one * own + lax.broadcasted_iota(jnp.int32, (own, head_dim), 0)
        )
        late = jnp.where(starts > position, 1.0, 0.0).astype(jnp.bfloat16)
        rows = slice(at * own, (at + 1) * own)
        for head in range(heads):
            marked_ref[head, rows, :head_dim] = q_refs[at][halves[at] * heads + head]
            marked_ref[head, rows, head_dim:] = late

    step, several = SOURCES[0]
    for at, turn in enumerate(several):
        rank = source_rank(plane_rank, step, turn)
        for here in range(slots_here):
            image = slot_image_ref[(rank * PLANE + member) * slots_here + here]
            put_slot(keys_ref, values_ref, at * slots_here + here, kv_ref, at, here, image)
    sums_ref[...] = jnp.zeros_like(sums_ref)
    column = lax.broadcasted_iota(jnp.int32, sums_ref.shape, 1)
    keys = keys_ref[...].reshape(-1, 2 * head_dim)
    values = values_ref[...].reshape(-1, 2 * head_dim)

    def one_head(head, _):
        total = weigh(marked_ref[head], keys, values, scale)
        at = pl.ds(pl.multiple_of(head * head_dim, head_dim), head_dim)
        numer_ref[:, at] = total[:, :head_dim].astype(numer_ref.dtype)
        sums_ref[...] = jnp.where(column == head, total[:, head_dim:], sums_ref[...])
        return 0

    lax.fori_loop(0, heads, one_head, 0, unroll=2)


def pack_slots(plan_ref, kv_refs, keys_ref, values_ref, group, slots_here):
    put = functools.partial(put_slot, keys_ref, values_ref)
    number = 0
    for kv_ref, (_, several) in zip(kv_refs, SOURCES[1:]):
        for at in range(len(several)):
            for here in range(slots_here):
                image, to = plan_ref[2 * number], plan_ref[2 * number + 1]
                pl.when(to >= 0)(functools.partial(put, to, kv_ref, at, here, image))
                number += 1
    kept = plan_ref[2 * number]

    def fill(to, _):
        put(to, kv_refs[0], 0, 0, NO_IMAGE)
        return 0

    lax.fori_loop(kept, (kept + group - 1) // group * group, fill, 0)


def attend_last_kernel(plan_ref, *refs, scale, group, slots_here, pack, first, together):
    numer_ref, came_ref, marked_ref = refs[:3]
    if pack:
        kv_refs, refs = refs[3 : 2 + len(SOURCES)], refs[2 + len(SOURCES) :]
        out_refs, (keys_ref, values_ref, sums_ref) = refs[:-3], refs[-3:]
        pack_slots(plan_ref, kv_refs, keys_ref, values_ref, group, slots_here)
    else:
        keys_ref, values_ref, *out_refs, sums_ref = refs[3:]
    heads, _, width = marked_ref.shape
    head_dim = width // 2
    count = sums_ref.shape[0]
    rows = slice(first, first + count)
    slots = keys_ref.shape[0]
    kept = plan_ref[2 * slots]
    turns = (kept + group - 1) // group
    sums_ref[...] = came_ref[rows]
    column = lax.broadcasted_iota(jnp.int32, sums_ref.shape, 1)

    def store(at, values):
        start = 0
        for out_ref in out_refs:
            stop = start + out_ref.shape[0]
            out_ref[:, at] = values[start:stop]
            start = stop

    def some_heads(number, _, packed):
        keys = keys_ref[:packed].reshape(-1, width)
        values = values_ref[:packed].reshape(-1, width)
        several = [number * together + i for i in range(together)]
        queries = jnp.concatenate([marked_ref[head, rows] for head in several], axis=0)
        totals = weigh(queries, keys, values, scale)
        sums = sums_ref[...]
        for i, head in enumerate(several):
            total = totals[count * i : count * (i + 1)]
            at = pl.ds(pl.multiple_of(head * head_dim, head_dim), head_dim)
            numer = numer_ref[rows, at].astype(jnp.float32) + total[:, :head_dim]
            store(at, numer.astype(jnp.bfloat16))
            sums = jnp.where(column == head, sums + total[:, head_dim:], sums)
        sums_ref[...] = sums
        return 0

    for turn in range(1, slots // group + 1):

        @pl.when(turns == turn)
        def _():
            lax.fori_loop(
                0,
                heads // together,
                functools.partial(some_heads, packed=turn * group),
                0,
                unroll=2,
            )

    @pl.when(turns == 0)
    def _():
        store(slice(0, heads * head_dim), numer_ref[rows])

    store(
        slice(heads * head_dim, (heads + 1) * head_dim),
        split_sums(sums_ref[...], heads).astype(jnp.bfloat16),
    )


def add_kernel(kept_ref, came_ref, out_ref, *, heads):
    own, width = out_ref.shape
    cut = width - 128
    for first in range(0, cut, 256):
        columns = slice(first, min(first + 256, cut))
        out_ref[:, columns] = (
            kept_ref[:, columns].astype(jnp.float32)
            + came_ref[own:, columns].astype(jnp.float32)
        ).astype(out_ref.dtype)
    sums = kept_ref[:, cut:].astype(jnp.float32) + came_ref[own:, cut:].astype(jnp.float32)
    out_ref[:, cut:] = split_sums(join_sums(sums, heads), heads).astype(out_ref.dtype)


def combine_kernel(image_start_ref, place_ref, gate_ref, kept_ref, core_ref, chip_ref, out_ref):
    own, out_width = out_ref.shape
    width = kept_ref.shape[1]
    head_dim = width - out_width
    heads = out_width // head_dim
    first = (place_ref[0] * PLANE + place_ref[1]) * own
    position = first + lax.broadcasted_iota(jnp.int32, (own, 1), 0)
    seen = position >= image_start_ref[0]
    factor = jnp.tanh(gate_ref[...])

    def total(columns):
        return (
            kept_ref[:, columns].astype(jnp.float32)
            + core_ref[:own, columns].astype(jnp.float32)
            + chip_ref[:, columns].astype(jnp.float32)
        )

    sums = join_sums(total(slice(out_width, width)), heads)
    share = jnp.where(seen, factor / jnp.where(seen, sums, 1.0), 0.0)
    for head in range(heads):
        columns = slice(head * head_dim, (head + 1) * head_dim)
        out_ref[:, columns] = (total(columns) * share[:, head : head + 1]).astype(out_ref.dtype)


def gather_along_z(block, beside=None):
    ctx_size = lax.axis_size("ctx")
    ranks = ctx_size // PLANE

    def shift(value, *distances):
        moves = [distances[i % len(distances)] * PLANE for i in range(ctx_size)]
        return lax.ppermute(
            value, "ctx", [(i, (i + moves[i]) % ctx_size) for i in range(ctx_size)]
        )

    groups = [
        [rank * PLANE + member for rank in range(first, ranks, STRIDE)]
        for member in range(PLANE)
        for first in range(STRIDE)
    ]
    own = lax.all_gather(block, "ctx", axis_index_groups=groups)
    if beside is not None:
        own, beside = lax.optimization_barrier((own, beside))
    return (own, shift(own, 2, -2), shift(own, 1), shift(own, -1)), beside


def other_member(value, mask):
    ctx_size = lax.axis_size("ctx")
    return lax.ppermute(value, "ctx", [(i, i ^ mask) for i in range(ctx_size)])


def local(
    queries,
    q_gain,
    k_gain,
    attn_gate,
    vision,
    key_projection_matrix,
    value_projection_matrix,
    image_start,
    slot_image,
):
    ctx_size = lax.axis_size("ctx")
    head_size = lax.axis_size("head")
    ranks = ctx_size // PLANE
    own_index = lax.axis_index("ctx")
    plane_rank = own_index // PLANE
    member = own_index % PLANE
    place = jnp.stack([plane_rank, member]).astype(jnp.int32)
    head_dim = q_gain.shape[0]
    tokens, q_cols = queries.shape
    heads = q_cols // head_dim
    rows, features = vision.shape
    piece_rows, kv_cols = key_projection_matrix.shape
    in_plane = [[rank * PLANE + m for m in range(PLANE)] for rank in range(ranks)]
    whole_plane = [
        [rank * PLANE * head_size + i for i in range(PLANE * head_size)] for rank in range(ranks)
    ]

    with jax.named_scope("norm_queries"):
        normed = pl.pallas_call(
            query_kernel,
            out_shape=jax.ShapeDtypeStruct((heads, tokens, head_dim), jnp.bfloat16),
            in_specs=[vmem(), vmem()],
            out_specs=vmem(),
            compiler_params=params(),
        )(queries, q_gain.reshape(1, head_dim))

    with jax.named_scope("spread_vision"):
        blocks = features // (piece_rows * PLANE)
        mine = pl.pallas_call(
            spread_kernel,
            out_shape=jax.ShapeDtypeStruct(
                (PLANE, head_size, blocks, rows, piece_rows), jnp.bfloat16
            ),
            in_specs=[vmem()],
            out_specs=pl.BlockSpec(memory_space=pltpu.HBM),
            scratch_shapes=[
                pltpu.VMEM((PLANE, head_size, blocks, rows, piece_rows), jnp.bfloat16),
                pltpu.SemaphoreType.DMA((PLANE,)),
            ],
            compiler_params=pltpu.CompilerParams(vmem_limit_bytes=SPREAD_LIMIT),
        )(vision)
        mine = mine.reshape(PLANE * head_size, blocks, rows, piece_rows)
        spread = lax.all_to_all(mine, ("ctx", "head"), 0, 0, axis_index_groups=whole_plane)
        spread = spread.reshape(PLANE, ranks, rows, piece_rows)

    with jax.named_scope("gather_projections"):
        weights, _ = gather_along_z(
            jnp.concatenate([key_projection_matrix, value_projection_matrix], axis=1)
        )

    with jax.named_scope("share_queries"):
        core_queries = other_member(normed, 1)
        spread, core_queries = lax.optimization_barrier((spread, core_queries))
        chip_queries = other_member(jnp.concatenate([normed, core_queries]), 2)

    with jax.named_scope("project"):
        partial = pl.pallas_call(
            project_first_kernel,
            out_shape=jax.ShapeDtypeStruct((PLANE * rows, 2 * kv_cols), jnp.float32),
            in_specs=[smem()] + [vmem()] * (1 + FIRST),
            out_specs=vmem(),
            compiler_params=params(),
        )(place, spread, *weights[:FIRST])
        triple = 3 * kv_cols
        shapes = [(rows, triple), (rows, triple), (2 * rows, triple)]
        kept, to_chip, to_core = pl.pallas_call(
            project_last_kernel,
            out_shape=[jax.ShapeDtypeStruct(shape, jnp.bfloat16) for shape in shapes],
            in_specs=[smem()] + [vmem()] * (2 + len(weights) - FIRST),
            out_specs=[vmem()] * 3,
            compiler_params=params(),
        )(place, spread, *weights[FIRST:], partial)

    with jax.named_scope("sum_projections"):
        from_core = other_member(to_core, 1)
        to_chip = pl.pallas_call(
            add_products_kernel,
            out_shape=jax.ShapeDtypeStruct((rows, triple), jnp.bfloat16),
            in_specs=[vmem()] * 2,
            out_specs=vmem(),
            compiler_params=params(),
        )(to_chip, from_core)
        from_chip = other_member(to_chip, 2)
        own_kv = pl.pallas_call(
            finish_kernel,
            out_shape=jax.ShapeDtypeStruct((rows, 2 * kv_cols), jnp.bfloat16),
            in_specs=[vmem()] * 4,
            out_specs=vmem(),
            compiler_params=params(),
        )(kept, from_core, from_chip, k_gain.reshape(1, head_dim))

    with jax.named_scope("gather_keys_values"):
        all_kv, chip_queries = gather_along_z(own_kv, chip_queries)

    with jax.named_scope("attend"):
        slots_here = slot_image.shape[0] // ctx_size
        tile_rows = rows // slots_here
        slots = slots_here * len(SOURCES[0][1])
        last_slots = ranks * slots_here - slots
        group = math.gcd(last_slots, 4)
        width = q_cols + head_dim
        scale = head_dim ** (-0.5) * math.log2(math.e)
        plane_queries = [(normed, 0), (chip_queries, 0), (core_queries, 0), (chip_queries, 1)]

        def cost(rows_here, slots):
            scores = heads * rows_here * slots * tile_rows
            return pl.CostEstimate(
                flops=8 * scores * head_dim,
                bytes_accessed=4 * rows_here * width,
                transcendentals=scores,
            )

        numer, sums, marked, plan = pl.pallas_call(
            functools.partial(
                attend_first_kernel,
                scale=scale,
                slots_here=slots_here,
                halves=tuple(half for _, half in plane_queries),
            ),
            out_shape=[
                jax.ShapeDtypeStruct((PLANE * tokens, q_cols), jnp.bfloat16),
                jax.ShapeDtypeStruct((PLANE * tokens, head_dim), jnp.float32),
                jax.ShapeDtypeStruct((heads, PLANE * tokens, 2 * head_dim), jnp.bfloat16),
                jax.ShapeDtypeStruct((2 * last_slots + 1,), jnp.int32),
            ],
            in_specs=[smem()] * 3 + [vmem()] * (1 + PLANE),
            out_specs=[vmem()] * 3 + [smem()],
            scratch_shapes=[pltpu.VMEM((slots, tile_rows, 2 * head_dim), jnp.bfloat16)] * 2,
            compiler_params=params(),
            cost_estimate=cost(PLANE * tokens, slots),
        )(
            image_start,
            slot_image,
            place,
            all_kv[0],
            *(source for source, _ in plane_queries),
        )
        block = jax.ShapeDtypeStruct((tokens, width), jnp.bfloat16)
        two_blocks = jax.ShapeDtypeStruct((2 * tokens, width), jnp.bfloat16)
        packed = jax.ShapeDtypeStruct((last_slots, tile_rows, 2 * head_dim), jnp.bfloat16)

        def attend_last(first, last, inputs, outputs, pack, together):
            return pl.pallas_call(
                functools.partial(
                    attend_last_kernel,
                    scale=scale,
                    group=group,
                    slots_here=slots_here,
                    pack=pack,
                    first=first * tokens,
                    together=together,
                ),
                out_shape=outputs,
                in_specs=[smem()] + [vmem()] * len(inputs),
                out_specs=[vmem()] * len(outputs),
                scratch_shapes=[pltpu.VMEM(((last - first) * tokens, head_dim), jnp.float32)],
                compiler_params=params(),
                cost_estimate=cost((last - first) * tokens, last_slots),
            )(plan, *inputs)

        to_chip, to_core, keys, values = attend_last(
            1,
            PLANE,
            (numer, sums, marked, *all_kv[1:]),
            [block, two_blocks, packed, packed],
            True,
            2,
        )

    with jax.named_scope("sum_attention"):
        from_core = other_member(to_core, 1)
        to_chip = pl.pallas_call(
            functools.partial(add_kernel, heads=heads),
            out_shape=block,
            in_specs=[vmem(), vmem()],
            out_specs=vmem(),
            compiler_params=params(),
        )(to_chip, from_core)
        to_chip, keys = lax.optimization_barrier((to_chip, keys))
        from_chip = other_member(to_chip, 2)
        [kept] = attend_last(0, 1, (numer, sums, marked, keys, values), [block], False, 4)
        return pl.pallas_call(
            combine_kernel,
            out_shape=jax.ShapeDtypeStruct((tokens, q_cols), jnp.bfloat16),
            in_specs=[smem(), smem()] + [vmem()] * 4,
            out_specs=vmem(),
            compiler_params=params(),
        )(image_start, place, attn_gate.reshape(1, 1), kept, from_core, from_chip)


def solution(mesh):
    in_specs = (
        P("ctx", "head"),
        P(),
        P(),
        P(),
        P("ctx", "head"),
        P("ctx", "head"),
        P("ctx", "head"),
        P(),
        P(),
    )
    out_specs = P("ctx", "head")
    return jax.shard_map(local, mesh=mesh, in_specs=in_specs, out_specs=out_specs, check_vma=False)
```

```python
import functools
import math

import jax
import jax.numpy as jnp
from jax import lax
from jax.experimental import pallas as pl
from jax.experimental.pallas import tpu as pltpu
from jax.sharding import PartitionSpec as P

EPS = 1e-05
PLANE = 4
VMEM_LIMIT = 16 * 1024 * 1024
TOKEN_ORDER = (0, 2, 1, 3)
SPREAD_LIMIT = 62 * 1024 * 1024
NO_IMAGE = 127
HIDE = -30000.0
STRIDE = 4
SOURCES = ((0, (0, 1, 2, 3)), (2, (0, 1, 2, 3)), (-1, (0, 1, 2, 3)), (1, (0, 1, 2, 3)))

FIRST = 2


def source_rank(plane_rank, step, turn):
    return lax.rem(plane_rank + step + STRIDE, STRIDE) + STRIDE * turn


def params(**more):
    return pltpu.CompilerParams(vmem_limit_bytes=VMEM_LIMIT, **more)


def vmem():
    return pl.BlockSpec(memory_space=pltpu.VMEM)


def smem():
    return pl.BlockSpec(memory_space=pltpu.SMEM)


def spread_kernel(x_ref, out_ref, pieces_ref, sems):
    members, peers, blocks, _, width = out_ref.shape
    copies = []
    for member in range(members):
        for block in range(blocks):
            first = (block * members + member) * width
            piece = x_ref[:, first : first + width]
            for peer in range(peers):
                pieces_ref[member, peer, block] = piece
        copies.append(
            pltpu.make_async_copy(pieces_ref.at[member], out_ref.at[member], sems.at[member])
        )
        copies[-1].start()
    for copy in copies:
        copy.wait()


def order_of(member):
    return member, member ^ 2, member ^ 1, member ^ 3


def products(place_ref, x_ref, weight_refs, sources):
    depth = x_ref.shape[3]
    total = None
    for ref, (step, several) in zip(weight_refs, sources):
        for at in range(0, len(several), 2):
            both = [source_rank(place_ref[0], step, several[at + i]) for i in range(2)]
            part = jnp.dot(
                jnp.concatenate(
                    [
                        jnp.concatenate([x_ref[member, rank] for rank in both], axis=1)
                        for member in order_of(place_ref[1])
                    ],
                    axis=0,
                ),
                ref[at : at + 2].reshape(2 * depth, ref.shape[2]),
                preferred_element_type=jnp.float32,
            )
            total = part if total is None else total + part
    return total


def project_first_kernel(place_ref, x_ref, *refs):
    refs[-1][...] = products(place_ref, x_ref, refs[:-1], SOURCES[:FIRST])


def pack_products(total):
    head_dim = total.shape[1] // 2
    keys = total[:, :head_dim]
    high = keys.astype(jnp.bfloat16)
    low = (keys - high.astype(jnp.float32)).astype(jnp.bfloat16)
    return jnp.concatenate([high, low, total[:, head_dim:].astype(jnp.bfloat16)], axis=1)


def unpack_products(parts):
    head_dim = parts.shape[1] // 3
    parts = parts.astype(jnp.float32)
    keys = parts[:, :head_dim] + parts[:, head_dim : 2 * head_dim]
    return jnp.concatenate([keys, parts[:, 2 * head_dim :]], axis=1)


def project_last_kernel(place_ref, x_ref, *refs):
    weight_refs, first_ref, out_refs = refs[:-4], refs[-4], refs[-3:]
    total = first_ref[...] + products(place_ref, x_ref, weight_refs, SOURCES[FIRST:])
    packed = pack_products(total)
    rows = x_ref.shape[2]
    for out_ref, (start, stop) in zip(out_refs, ((0, 1), (1, 2), (2, 4))):
        out_ref[...] = packed[start * rows : stop * rows]


def add_products_kernel(kept_ref, came_ref, out_ref):
    rows = kept_ref.shape[0]
    out_ref[...] = pack_products(
        unpack_products(kept_ref[...]) + unpack_products(came_ref[rows:])
    )


def finish_kernel(kept_ref, core_ref, chip_ref, gain_ref, out_ref):
    rows = kept_ref.shape[0]
    raw = (
        unpack_products(kept_ref[...])
        + unpack_products(core_ref[:rows])
        + unpack_products(chip_ref[...])
    )
    head_dim = gain_ref.shape[1]
    keys = raw[:, :head_dim]
    mean = jnp.mean(keys * keys, axis=-1, keepdims=True)
    keys = keys * lax.rsqrt(mean + EPS) * gain_ref[...]
    out_ref[...] = jnp.concatenate([keys, raw[:, head_dim:]], axis=1).astype(out_ref.dtype)


def query_kernel(q_ref, gain_ref, out_ref):
    heads, _, head_dim = out_ref.shape
    for head in range(heads):
        raw = q_ref[:, head * head_dim : (head + 1) * head_dim].astype(jnp.float32)
        mean = jnp.mean(raw * raw, axis=-1, keepdims=True)
        out_ref[head] = (raw * lax.rsqrt(mean + EPS) * gain_ref[...]).astype(out_ref.dtype)


def split_sums(sums, heads):
    column = lax.broadcasted_iota(jnp.int32, sums.shape, 1)
    high = sums.astype(jnp.bfloat16).astype(jnp.float32)
    low = pltpu.roll(sums - high, heads, 1)
    return jnp.where(column < heads, high, jnp.where(column < 2 * heads, low, 0.0))


def join_sums(parts, heads):
    return parts + pltpu.roll(parts, parts.shape[1] - heads, 1)


def put_slot(keys_ref, values_ref, to, kv_ref, at, here, image):
    _, tile_rows, width = keys_ref.shape
    head_dim = width // 2
    rows = slice(here * tile_rows, (here + 1) * tile_rows)
    lane = lax.broadcasted_iota(jnp.int32, (tile_rows, head_dim), 1)
    mark = jnp.where(lane == image, HIDE, 0.0).astype(jnp.bfloat16)
    ones = jnp.ones((tile_rows, head_dim), jnp.bfloat16)
    keys_ref[to] = jnp.concatenate([kv_ref[at, rows, :head_dim], mark], axis=1)
    values_ref[to] = jnp.concatenate([kv_ref[at, rows, head_dim:], ones], axis=1)


def weigh(queries, keys, values, scale):
    scores = lax.dot_general(
        queries, keys, (((1,), (1,)), ((), ())), preferred_element_type=jnp.float32
    )
    weights = jnp.exp2(scores * scale).astype(jnp.bfloat16)
    return jnp.dot(weights, values, preferred_element_type=jnp.float32)


def attend_first_kernel(
    image_start_ref, slot_image_ref, place_ref, *refs, scale, slots_here, halves
):
    kv_ref, q_refs = refs[0], refs[1 : 1 + PLANE]
    numer_ref, sums_ref, marked_ref, plan_ref, keys_ref, values_ref = refs[1 + PLANE :]
    _, own, head_dim = q_refs[0].shape
    heads = marked_ref.shape[0]
    n_images = image_start_ref.shape[0]
    tokens = PLANE * own
    plane_rank = place_ref[0]
    member = place_ref[1]
    first_token = plane_rank * tokens
    total_tokens = tokens * (slot_image_ref.shape[0] // (slots_here * PLANE))

    kept = jnp.int32(0)
    number = 0
    for step, several in SOURCES[1:]:
        for turn in several:
            rank = source_rank(plane_rank, step, turn)
            for here in range(slots_here):
                image = slot_image_ref[(rank * PLANE + member) * slots_here + here]
                start = image_start_ref[jnp.minimum(image, n_images - 1)]
                seen = jnp.logical_and(image < n_images, start < first_token + tokens)
                plan_ref[2 * number] = image
                plan_ref[2 * number + 1] = jnp.where(seen, kept, -1)
                kept = kept + seen.astype(jnp.int32)
                number += 1
    plan_ref[2 * number] = kept

    lane = lax.broadcasted_iota(jnp.int32, (own, head_dim), 1)
    starts = jnp.full((own, head_dim), total_tokens, jnp.int32)
    for image in range(n_images):
        starts = jnp.where(lane == image, image_start_ref[image], starts)
    for at, mask in enumerate(TOKEN_ORDER):
        one = member ^ mask
        position = (
            first_token + one * own + lax.broadcasted_iota(jnp.int32, (own, head_dim), 0)
        )
        late = jnp.where(starts > position, 1.0, 0.0).astype(jnp.bfloat16)
        rows = slice(at * own, (at + 1) * own)
        for head in range(heads):
            marked_ref[head, rows, :head_dim] = q_refs[at][halves[at] * heads + head]
            marked_ref[head, rows, head_dim:] = late

    step, several = SOURCES[0]
    for at, turn in enumerate(several):
        rank = source_rank(plane_rank, step, turn)
        for here in range(slots_here):
            image = slot_image_ref[(rank * PLANE + member) * slots_here + here]
            put_slot(keys_ref, values_ref, at * slots_here + here, kv_ref, at, here, image)
    sums_ref[...] = jnp.zeros_like(sums_ref)
    column = lax.broadcasted_iota(jnp.int32, sums_ref.shape, 1)
    keys = keys_ref[...].reshape(-1, 2 * head_dim)
    values = values_ref[...].reshape(-1, 2 * head_dim)

    def one_head(head, _):
        total = weigh(marked_ref[head], keys, values, scale)
        at = pl.ds(pl.multiple_of(head * head_dim, head_dim), head_dim)
        numer_ref[:, at] = total[:, :head_dim].astype(numer_ref.dtype)
        sums_ref[...] = jnp.where(column == head, total[:, head_dim:], sums_ref[...])
        return 0

    lax.fori_loop(0, heads, one_head, 0, unroll=2)


def pack_slots(plan_ref, kv_refs, keys_ref, values_ref, group, slots_here):
    put = functools.partial(put_slot, keys_ref, values_ref)
    number = 0
    for kv_ref, (_, several) in zip(kv_refs, SOURCES[1:]):
        for at in range(len(several)):
            for here in range(slots_here):
                image, to = plan_ref[2 * number], plan_ref[2 * number + 1]
                pl.when(to >= 0)(functools.partial(put, to, kv_ref, at, here, image))
                number += 1
    kept = plan_ref[2 * number]

    def fill(to, _):
        put(to, kv_refs[0], 0, 0, NO_IMAGE)
        return 0

    lax.fori_loop(kept, (kept + group - 1) // group * group, fill, 0)


def attend_last_kernel(plan_ref, *refs, scale, group, slots_here, pack, first, together):
    numer_ref, came_ref, marked_ref = refs[:3]
    if pack:
        kv_refs, refs = refs[3 : 2 + len(SOURCES)], refs[2 + len(SOURCES) :]
        out_refs, (keys_ref, values_ref, sums_ref) = refs[:-3], refs[-3:]
        pack_slots(plan_ref, kv_refs, keys_ref, values_ref, group, slots_here)
    else:
        keys_ref, values_ref, *out_refs, sums_ref = refs[3:]
    heads, _, width = marked_ref.shape
    head_dim = width // 2
    count = sums_ref.shape[0]
    rows = slice(first, first + count)
    slots = keys_ref.shape[0]
    kept = plan_ref[2 * slots]
    turns = (kept + group - 1) // group
    sums_ref[...] = came_ref[rows]
    column = lax.broadcasted_iota(jnp.int32, sums_ref.shape, 1)

    def store(at, values):
        start = 0
        for out_ref in out_refs:
            stop = start + out_ref.shape[0]
            out_ref[:, at] = values[start:stop]
            start = stop

    def some_heads(number, _, packed):
        keys = keys_ref[:packed].reshape(-1, width)
        values = values_ref[:packed].reshape(-1, width)
        several = [number * together + i for i in range(together)]
        queries = jnp.concatenate([marked_ref[head, rows] for head in several], axis=0)
        totals = weigh(queries, keys, values, scale)
        sums = sums_ref[...]
        for i, head in enumerate(several):
            total = totals[count * i : count * (i + 1)]
            at = pl.ds(pl.multiple_of(head * head_dim, head_dim), head_dim)
            numer = numer_ref[rows, at].astype(jnp.float32) + total[:, :head_dim]
            store(at, numer.astype(jnp.bfloat16))
            sums = jnp.where(column == head, sums + total[:, head_dim:], sums)
        sums_ref[...] = sums
        return 0

    for turn in range(1, slots // group + 1):

        @pl.when(turns == turn)
        def _():
            lax.fori_loop(
                0,
                heads // together,
                functools.partial(some_heads, packed=turn * group),
                0,
                unroll=2 if pack else 1,
            )

    @pl.when(turns == 0)
    def _():
        store(slice(0, heads * head_dim), numer_ref[rows])

    store(
        slice(heads * head_dim, (heads + 1) * head_dim),
        split_sums(sums_ref[...], heads).astype(jnp.bfloat16),
    )


def add_kernel(kept_ref, came_ref, out_ref, *, heads):
    own, width = out_ref.shape
    cut = width - 128
    for first in range(0, cut, 256):
        columns = slice(first, min(first + 256, cut))
        out_ref[:, columns] = (
            kept_ref[:, columns].astype(jnp.float32)
            + came_ref[own:, columns].astype(jnp.float32)
        ).astype(out_ref.dtype)
    sums = kept_ref[:, cut:].astype(jnp.float32) + came_ref[own:, cut:].astype(jnp.float32)
    out_ref[:, cut:] = split_sums(join_sums(sums, heads), heads).astype(out_ref.dtype)


def combine_kernel(
    image_start_ref, place_ref, gate_ref, kept_ref, core_ref, chip_ref, out_ref, done_ref, sems
):
    own, out_width = out_ref.shape
    width = kept_ref.shape[1]
    head_dim = width - out_width
    heads = out_width // head_dim
    first = (place_ref[0] * PLANE + place_ref[1]) * own
    position = first + lax.broadcasted_iota(jnp.int32, (own, 1), 0)
    seen = position >= image_start_ref[0]
    factor = jnp.tanh(gate_ref[...])

    def total(columns):
        return (
            kept_ref[:, columns].astype(jnp.float32)
            + core_ref[:own, columns].astype(jnp.float32)
            + chip_ref[:, columns].astype(jnp.float32)
        )

    sums = join_sums(total(slice(out_width, width)), heads)
    share = jnp.where(seen, factor / jnp.where(seen, sums, 1.0), 0.0)
    copies = []
    step = 2
    for head in range(heads):
        columns = slice(head * head_dim, (head + 1) * head_dim)
        done_ref[:, columns] = (total(columns) * share[:, head : head + 1]).astype(done_ref.dtype)
        if head % step == step - 1:
            several = slice((head + 1 - step) * head_dim, (head + 1) * head_dim)
            copies.append(
                pltpu.make_async_copy(
                    done_ref.at[:, several], out_ref.at[:, several], sems.at[head // step]
                )
            )
            copies[-1].start()
    for copy in copies:
        copy.wait()


def gather_along_z(block, beside=None):
    ctx_size = lax.axis_size("ctx")
    ranks = ctx_size // PLANE

    def shift(value, *distances):
        moves = [distances[i % len(distances)] * PLANE for i in range(ctx_size)]
        return lax.ppermute(
            value, "ctx", [(i, (i + moves[i]) % ctx_size) for i in range(ctx_size)]
        )

    groups = [
        [rank * PLANE + member for rank in range(first, ranks, STRIDE)]
        for member in range(PLANE)
        for first in range(STRIDE)
    ]
    own = lax.all_gather(block, "ctx", axis_index_groups=groups)
    if beside is not None:
        own, beside = lax.optimization_barrier((own, beside))
    return (own, shift(own, 2, -2), shift(own, 1), shift(own, -1)), beside


def other_member(value, mask):
    ctx_size = lax.axis_size("ctx")
    return lax.ppermute(value, "ctx", [(i, i ^ mask) for i in range(ctx_size)])


def local(
    queries,
    q_gain,
    k_gain,
    attn_gate,
    vision,
    key_projection_matrix,
    value_projection_matrix,
    image_start,
    slot_image,
):
    ctx_size = lax.axis_size("ctx")
    head_size = lax.axis_size("head")
    ranks = ctx_size // PLANE
    own_index = lax.axis_index("ctx")
    plane_rank = own_index // PLANE
    member = own_index % PLANE
    place = jnp.stack([plane_rank, member]).astype(jnp.int32)
    head_dim = q_gain.shape[0]
    tokens, q_cols = queries.shape
    heads = q_cols // head_dim
    rows, features = vision.shape
    piece_rows, kv_cols = key_projection_matrix.shape
    in_plane = [[rank * PLANE + m for m in range(PLANE)] for rank in range(ranks)]
    whole_plane = [
        [rank * PLANE * head_size + i for i in range(PLANE * head_size)] for rank in range(ranks)
    ]

    with jax.named_scope("norm_queries"):
        normed = pl.pallas_call(
            query_kernel,
            out_shape=jax.ShapeDtypeStruct((heads, tokens, head_dim), jnp.bfloat16),
            in_specs=[vmem(), vmem()],
            out_specs=vmem(),
            compiler_params=params(),
        )(queries, q_gain.reshape(1, head_dim))

    with jax.named_scope("spread_vision"):
        blocks = features // (piece_rows * PLANE)
        mine = pl.pallas_call(
            spread_kernel,
            out_shape=jax.ShapeDtypeStruct(
                (PLANE, head_size, blocks, rows, piece_rows), jnp.bfloat16
            ),
            in_specs=[vmem()],
            out_specs=pl.BlockSpec(memory_space=pltpu.HBM),
            scratch_shapes=[
                pltpu.VMEM((PLANE, head_size, blocks, rows, piece_rows), jnp.bfloat16),
                pltpu.SemaphoreType.DMA((PLANE,)),
            ],
            compiler_params=pltpu.CompilerParams(vmem_limit_bytes=SPREAD_LIMIT),
        )(vision)
        mine = mine.reshape(PLANE * head_size, blocks, rows, piece_rows)
        spread = lax.all_to_all(mine, ("ctx", "head"), 0, 0, axis_index_groups=whole_plane)
        spread = spread.reshape(PLANE, ranks, rows, piece_rows)

    with jax.named_scope("gather_projections"):
        weights, _ = gather_along_z(
            jnp.concatenate([key_projection_matrix, value_projection_matrix], axis=1)
        )

    with jax.named_scope("share_queries"):
        core_queries = other_member(normed, 1)
        spread, core_queries = lax.optimization_barrier((spread, core_queries))
        chip_queries = other_member(jnp.concatenate([normed, core_queries]), 2)

    with jax.named_scope("project"):
        partial = pl.pallas_call(
            project_first_kernel,
            out_shape=jax.ShapeDtypeStruct((PLANE * rows, 2 * kv_cols), jnp.float32),
            in_specs=[smem()] + [vmem()] * (1 + FIRST),
            out_specs=vmem(),
            compiler_params=params(),
        )(place, spread, *weights[:FIRST])
        triple = 3 * kv_cols
        shapes = [(rows, triple), (rows, triple), (2 * rows, triple)]
        kept, to_chip, to_core = pl.pallas_call(
            project_last_kernel,
            out_shape=[jax.ShapeDtypeStruct(shape, jnp.bfloat16) for shape in shapes],
            in_specs=[smem()] + [vmem()] * (2 + len(weights) - FIRST),
            out_specs=[vmem()] * 3,
            compiler_params=params(),
        )(place, spread, *weights[FIRST:], partial)

    with jax.named_scope("sum_projections"):
        from_core = other_member(to_core, 1)
        to_chip = pl.pallas_call(
            add_products_kernel,
            out_shape=jax.ShapeDtypeStruct((rows, triple), jnp.bfloat16),
            in_specs=[vmem()] * 2,
            out_specs=vmem(),
            compiler_params=params(),
        )(to_chip, from_core)
        from_chip = other_member(to_chip, 2)
        own_kv = pl.pallas_call(
            finish_kernel,
            out_shape=jax.ShapeDtypeStruct((rows, 2 * kv_cols), jnp.bfloat16),
            in_specs=[vmem()] * 4,
            out_specs=vmem(),
            compiler_params=params(),
        )(kept, from_core, from_chip, k_gain.reshape(1, head_dim))

    with jax.named_scope("gather_keys_values"):
        all_kv, chip_queries = gather_along_z(own_kv, chip_queries)

    with jax.named_scope("attend"):
        slots_here = slot_image.shape[0] // ctx_size
        tile_rows = rows // slots_here
        slots = slots_here * len(SOURCES[0][1])
        last_slots = ranks * slots_here - slots
        group = math.gcd(last_slots, 4)
        width = q_cols + head_dim
        scale = head_dim ** (-0.5) * math.log2(math.e)
        plane_queries = [(normed, 0), (chip_queries, 0), (core_queries, 0), (chip_queries, 1)]

        def cost(rows_here, slots):
            scores = heads * rows_here * slots * tile_rows
            return pl.CostEstimate(
                flops=8 * scores * head_dim,
                bytes_accessed=4 * rows_here * width,
                transcendentals=scores,
            )

        numer, sums, marked, plan = pl.pallas_call(
            functools.partial(
                attend_first_kernel,
                scale=scale,
                slots_here=slots_here,
                halves=tuple(half for _, half in plane_queries),
            ),
            out_shape=[
                jax.ShapeDtypeStruct((PLANE * tokens, q_cols), jnp.bfloat16),
                jax.ShapeDtypeStruct((PLANE * tokens, head_dim), jnp.float32),
                jax.ShapeDtypeStruct((heads, PLANE * tokens, 2 * head_dim), jnp.bfloat16),
                jax.ShapeDtypeStruct((2 * last_slots + 1,), jnp.int32),
            ],
            in_specs=[smem()] * 3 + [vmem()] * (1 + PLANE),
            out_specs=[vmem()] * 3 + [smem()],
            scratch_shapes=[pltpu.VMEM((slots, tile_rows, 2 * head_dim), jnp.bfloat16)] * 2,
            compiler_params=params(),
            cost_estimate=cost(PLANE * tokens, slots),
        )(
            image_start,
            slot_image,
            place,
            all_kv[0],
            *(source for source, _ in plane_queries),
        )
        block = jax.ShapeDtypeStruct((tokens, width), jnp.bfloat16)
        two_blocks = jax.ShapeDtypeStruct((2 * tokens, width), jnp.bfloat16)
        packed = jax.ShapeDtypeStruct((last_slots, tile_rows, 2 * head_dim), jnp.bfloat16)

        def attend_last(first, last, inputs, outputs, pack, together):
            return pl.pallas_call(
                functools.partial(
                    attend_last_kernel,
                    scale=scale,
                    group=group,
                    slots_here=slots_here,
                    pack=pack,
                    first=first * tokens,
                    together=together,
                ),
                out_shape=outputs,
                in_specs=[smem()] + [vmem()] * len(inputs),
                out_specs=[vmem()] * len(outputs),
                scratch_shapes=[pltpu.VMEM(((last - first) * tokens, head_dim), jnp.float32)],
                compiler_params=params(),
                cost_estimate=cost((last - first) * tokens, last_slots),
            )(plan, *inputs)

        to_chip, to_core, keys, values = attend_last(
            1,
            PLANE,
            (numer, sums, marked, *all_kv[1:]),
            [block, two_blocks, packed, packed],
            True,
            2,
        )

    with jax.named_scope("sum_attention"):
        from_core = other_member(to_core, 1)
        to_chip = pl.pallas_call(
            functools.partial(add_kernel, heads=heads),
            out_shape=block,
            in_specs=[vmem(), vmem()],
            out_specs=vmem(),
            compiler_params=params(),
        )(to_chip, from_core)
        to_chip, keys = lax.optimization_barrier((to_chip, keys))
        from_chip = other_member(to_chip, 2)
        [kept] = attend_last(0, 1, (numer, sums, marked, keys, values), [block], False, 4)
        return pl.pallas_call(
            combine_kernel,
            out_shape=jax.ShapeDtypeStruct((tokens, q_cols), jnp.bfloat16),
            in_specs=[smem(), smem()] + [vmem()] * 4,
            out_specs=pl.BlockSpec(memory_space=pltpu.HBM),
            scratch_shapes=[
                pltpu.VMEM((tokens, q_cols), jnp.bfloat16),
                pltpu.SemaphoreType.DMA((heads // 2,)),
            ],
            compiler_params=params(),
        )(image_start, place, attn_gate.reshape(1, 1), kept, from_core, from_chip)


def solution(mesh):
    in_specs = (
        P("ctx", "head"),
        P(),
        P(),
        P(),
        P("ctx", "head"),
        P("ctx", "head"),
        P("ctx", "head"),
        P(),
        P(),
    )
    out_specs = P("ctx", "head")
    return jax.shard_map(local, mesh=mesh, in_specs=in_specs, out_specs=out_specs, check_vma=False)
```
